32 devices in a mesh: gx: 16 (over z, x, core), gy: 2 (over y).
Axes of the slice: x: 2, y: 2, z: 4, core: 2. Of those that a mesh axis runs over, the one named last changes fastest.
Arguments:
- checkpoint: float32 [19, 128, 512], P(None, 'gx', 'gy'), as said below
- cotangent: float32 [19, 128, 512], P(None, 'gx', 'gy'), may hold values from -6 to 6
- blade_area: float32 [1536], replicated, may hold values from 0.5 to 2
- hub_tile: int32 [16], replicated, may hold values from 0 to 31
- point_side: int32 [1536], replicated, may hold values from 0 to 8
- point_local: int32 [1536], replicated, may hold values from 0 to 2047
Outputs:
- grad_checkpoint: float32 [19, 128, 512], P(None, 'gx', 'gy')
- grad_area: float32 [1536], replicated
The draws below stay inside these ranges and needn't reach their ends.
Inputs may be any that keep to these rules, and one draw needn't show every extreme that they name: `hub_tile`: tile ids count every tile of the slab. `point_side`: every actuator point lies in its hub tile or one of the eight tiles around it. `checkpoint`: populations are positive and near a local equilibrium with density near one and streamwise velocity near 0.08.
All inputs are finite; a program needn't handle non-finite values.
Results may differ from the reference program's by a relative error of at most 0.0003.
Values sent between devices are 32-bit elements; how exact they have to be, the bound alone decides.
A program may use at most 128 MiB of HBM per device.

```python
import math
import jax
import jax.numpy as jnp
import numpy as np
from jax import lax

CX = 8
CY = 16
NZ = 16
STEPS = 4
NTURB = 16
PTS = 96
NX = 128
NY = 32
NPTS = 1536
N_GX = 16
N_GY = 2


def draw_lattice():
    axis_part = [(1, 0, 0), (-1, 0, 0), (0, 1, 0), (0, -1, 0), (0, 0, 1), (0, 0, -1)]
    edge_part = [(1, 1, 0), (-1, -1, 0), (1, -1, 0), (-1, 1, 0), (1, 0, 1), (-1, 0, -1), (1, 0, -1), (-1, 0, 1), (0, 1, 1), (0, -1, -1), (0, 1, -1), (0, -1, 1)]
    vectors = np.array([(0, 0, 0)] + axis_part + edge_part) * 1.0
    weights = np.array([1.0 / 3.0] + [1.0 / 18.0] * 6 + [1.0 / 36.0] * 12)
    return (jnp.asarray(vectors, jnp.float32), jnp.asarray(weights, jnp.float32))


def draw_checkpoint(key, part):
    vectors, weights = draw_lattice()
    keys = jax.random.split(key, 5)
    shape = (NX, NY * NZ)
    noises = [jnp.clip(jax.random.normal(keys[column], shape, jnp.float32), -3.0, 3.0) for column in range(4)]
    baseline = 0.08
    perturb = 0.1 * jnp.clip(jax.random.normal(keys[4], (19,) + shape, jnp.float32), -2.0, 2.0)
    density = 1.0 + 0.04 * noises[0]
    velocity_x = baseline + 0.03 * noises[1]
    velocity_y = 0.03 * noises[2]
    velocity_z = 0.02 * noises[3]
    project = vectors[:, 0, None, None] * velocity_x[None] + vectors[:, 1, None, None] * velocity_y[None] + vectors[:, 2, None, None] * velocity_z[None]
    speed_sq = velocity_x * velocity_x + velocity_y * velocity_y + velocity_z * velocity_z
    equil = weights[:, None, None] * density[None] * (1.0 + 3.0 * project + 4.5 * project * project - 1.5 * speed_sq[None])
    return (equil * (1.0 + perturb)).astype(jnp.float32)


def place_ends(entries, stream_key, smallest, high):
    place = [jax.random.randint(jax.random.fold_in(stream_key, axis), (), 0, length) for axis, length in enumerate(entries.shape)]
    longest = entries.shape.index(max(entries.shape))
    neighbour = place[:longest] + [(place[longest] + 1) % entries.shape[longest]] + place[longest + 1:]
    return entries.at[tuple(place)].set(smallest).at[tuple(neighbour)].set(high)


def shard_levels(rng, shape, cuts, smallest, high):
    gain = 1.0
    for dim, blocks in cuts:
        draws = jax.random.uniform(jax.random.fold_in(jax.random.fold_in(rng, 6), dim), (blocks,), jnp.float32, smallest / len(cuts), high / len(cuts))
        gain = gain * jnp.repeat(jnp.exp(draws), shape[dim] // blocks).reshape((-1,) + (1,) * (len(shape) - 1 - dim))
    return gain


def bell_draw(stream_key, shape, scale, bound, cuts=(), held_as=jnp.bfloat16):
    values = jax.random.normal(stream_key, shape, jnp.float32) * scale
    if len(cuts) > 0:
        values = shard_levels(stream_key, shape, cuts, -0.22, 0.18) * values
    return jnp.clip(values, min=-bound, max=bound).astype(held_as)


def setup_inputs(seed: int = 0) -> dict:
    key_list = jax.random.split(jax.random.key(seed), 7)
    checkpoint = draw_checkpoint(jax.random.fold_in(key_list[6], 71), 0)
    cotangent = bell_draw(key_list[1], (19, NX, NY * NZ), 1.0, 6.0, ((1, 16), (2, 2)), jnp.float32)
    blade_area = jnp.clip(jnp.exp(jax.random.uniform(key_list[2], (NPTS,), jnp.float32, math.log(0.5), math.log(2.0))), 0.5, 2.0)
    hub_tile = place_ends(jax.random.randint(key_list[3], (NTURB,), 0, N_GX * N_GY), jax.random.fold_in(key_list[3], 1), 0, (N_GX * N_GY) - 1).astype(jnp.int32)
    point_side = place_ends(jax.random.randint(key_list[4], (NPTS,), 0, 9), jax.random.fold_in(key_list[4], 1), 0, 8).astype(jnp.int32)
    point_local = place_ends(jax.random.randint(key_list[5], (NPTS,), 0, CX * CY * NZ), jax.random.fold_in(key_list[5], 1), 0, (CX * CY * NZ) - 1).astype(jnp.int32)
    return {"checkpoint": checkpoint, "cotangent": cotangent, "blade_area": blade_area, "hub_tile": hub_tile, "point_side": point_side, "point_local": point_local}


TAU_ZERO = 0.52
SMAGORINSKY = 0.17 * 0.17
TINY = 1e-10
THRUST = 4.0
GHOST_RATES = np.array([1.05, 1.15, 1.25, 1.35, 1.45, 1.55, 1.65, 1.75, 1.85])

def lattice():
    axis_part = [(1, 0, 0), (-1, 0, 0), (0, 1, 0), (0, -1, 0), (0, 0, 1), (0, 0, -1)]
    edge_part = [(1, 1, 0), (-1, -1, 0), (1, -1, 0), (-1, 1, 0), (1, 0, 1), (-1, 0, -1), (1, 0, -1), (-1, 0, 1), (0, 1, 1), (0, -1, -1), (0, 1, -1), (0, -1, 1)]
    vectors = np.array([(0, 0, 0)] + axis_part + edge_part) * 1.0
    weights = np.array([1.0 / 3.0] + [1.0 / 18.0] * 6 + [1.0 / 36.0] * 12)
    opposite = np.array([int(np.argmin(np.abs(vectors + vectors[column]).sum(1))) for column in range(19)])
    return (vectors, weights, opposite)

def orthonormal(monomials, weights):
    rows = []
    for entry in monomials:
        vector = entry * 1.0
        for sweep in range(2):
            for other in rows:
                vector = vector - np.sum(weights * vector * other) * other
        vector = vector / np.sqrt(np.sum(weights * vector * vector))
        rows.append(vector)
    return np.stack(rows, 0)

def tables():
    vectors, weights, opposite = lattice()
    along_x, along_y, along_z = (vectors[:, 0], vectors[:, 1], vectors[:, 2])
    monomials = [np.ones(19), along_x, along_y, along_z, along_x * along_x, along_y * along_y, along_z * along_z, along_x * along_y, along_x * along_z, along_y * along_z, along_x * along_y * along_y, along_x * along_z * along_z, along_y * along_x * along_x, along_y * along_z * along_z, along_z * along_x * along_x, along_z * along_y * along_y, along_x * along_x * along_y * along_y, along_x * along_x * along_z * along_z, along_y * along_y * along_z * along_z]
    basis = orthonormal(monomials, weights)
    second = weights[:, None] * basis[4:10].T
    ghost = weights[:, None] * basis[10:].T * GHOST_RATES[None, :]
    stress = np.stack([along_x * along_x, along_y * along_y, along_z * along_z, along_x * along_y, along_x * along_z, along_y * along_z], 0)
    push = 3.0 * weights * along_x
    return {'vectors': vectors, 'weights': weights, 'opposite': opposite, 'high': jnp.asarray(basis[4:], jnp.float32), 'second': jnp.asarray(second, jnp.float32), 'ghost': jnp.asarray(ghost, jnp.float32), 'stress': jnp.asarray(stress, jnp.float32), 'push': jnp.asarray(push, jnp.float32), 'velt': jnp.asarray(vectors.T, jnp.float32), 'wvec': jnp.asarray(weights, jnp.float32), 'vecs': jnp.asarray(vectors, jnp.float32)}

def streamwise_velocity(flat, table):
    density = lax.optimization_barrier(jnp.sum(flat, 0))
    momentum = jnp.dot(table['velt'], flat, precision=lax.Precision.HIGHEST)
    return momentum[0] / density

def collide(flat, force, table):
    density = lax.optimization_barrier(jnp.sum(flat, 0))
    momentum = jnp.dot(table['velt'], flat, precision=lax.Precision.HIGHEST)
    velocity = momentum / density[None, :]
    project = jnp.dot(table['vecs'], velocity, precision=lax.Precision.HIGHEST)
    speed_sq = lax.optimization_barrier(jnp.sum(velocity * velocity, 0))
    equil = table['wvec'][:, None] * density[None, :] * (1.0 + 3.0 * project + 4.5 * project * project - 1.5 * speed_sq[None, :])
    noneq = flat - equil
    stress = jnp.dot(table['stress'], noneq, precision=lax.Precision.HIGHEST)
    square = lax.optimization_barrier(jnp.sum(stress[:3] * stress[:3], 0)) + 2.0 * lax.optimization_barrier(jnp.sum(stress[3:] * stress[3:], 0))
    relax_time = 0.5 * (TAU_ZERO + jnp.sqrt(TAU_ZERO * TAU_ZERO + 18.0 * SMAGORINSKY * jnp.sqrt(square + TINY) / density))
    moments = jnp.dot(table['high'], noneq, precision=lax.Precision.HIGHEST)
    relaxed = jnp.dot(table['second'], moments[:6] / relax_time[None, :], precision=lax.Precision.HIGHEST)
    relaxed = relaxed + jnp.dot(table['ghost'], moments[6:], precision=lax.Precision.HIGHEST)
    return flat - relaxed + table['push'][:, None] * force[None, :]

def wall_mask(vectors, depth):
    keep = np.ones((19, depth))
    for column in range(19):
        if vectors[column, 2] > 0.5:
            keep[column, 0] = 0.0
        if vectors[column, 2] < -0.5:
            keep[column, depth - 1] = 0.0
    return keep

def reference(checkpoint, cotangent, blade_area, hub_tile, point_side, point_local):
    table = tables()
    vectors = table['vectors']
    opposite = table['opposite']
    keep = jnp.asarray(wall_mask(vectors, NZ), jnp.float32)[:, None, None, :]
    turbine = jnp.arange(NTURB * PTS, dtype=jnp.int32) // PTS
    hub_x = hub_tile // N_GY
    hub_y = hub_tile % N_GY
    tile_x = (hub_x[turbine] + point_side // 3 - 1) % N_GX
    tile_y = (hub_y[turbine] + point_side % 3 - 1) % N_GY
    local_x = point_local // (CY * NZ)
    local_y = point_local // NZ % CY
    local_z = point_local % NZ
    cell = (((tile_x * CX + local_x) * NY + tile_y * CY + local_y) * NZ + local_z).astype(jnp.int32)

    def advance(state, area):
        field = state.reshape(19, NX, NY, NZ)
        pulled = jnp.stack([jnp.roll(field[column], (int(vectors[column, 0]), int(vectors[column, 1]), int(vectors[column, 2])), (0, 1, 2)) for column in range(19)], 0)
        read = pulled * keep + (1.0 - keep) * field[opposite]
        flat = read.reshape(19, NX * NY * NZ)
        sampled = streamwise_velocity(flat, table)[cell]
        numer = lax.optimization_barrier(jnp.sum((area * sampled).reshape(NTURB, PTS), 1))
        rotor = numer / lax.optimization_barrier(jnp.sum(area.reshape(NTURB, PTS), 1))
        thrust = -THRUST * area * rotor[turbine] * sampled
        force = jnp.zeros((NX * NY * NZ,), jnp.float32).at[cell].add(thrust)
        return collide(flat, force, table).reshape(19, NX, NY * NZ)

    def run(state, area):
        for counter in range(STEPS):
            state = jax.checkpoint(advance)(state, area)
        return state
    final, pullback = jax.vjp(run, checkpoint, blade_area)
    grads = pullback(cotangent)
    return (grads[0], grads[1])
```

```python
import functools

import jax
import jax.numpy as jnp
import numpy as np
from jax import lax
from jax.experimental import pallas as pl
from jax.experimental.pallas import tpu as pltpu
from jax.sharding import PartitionSpec as P

NZ = 16
STEPS = 4
NTURB = 16
PTS = 96
LANES = 128
SUBCELLS = 4

TAU_ZERO = 0.52
SMAGORINSKY = 0.17 * 0.17
TINY = 1e-10
THRUST = 4.0
GHOST_RATES = np.array([1.05, 1.15, 1.25, 1.35, 1.45, 1.55, 1.65, 1.75, 1.85])
MESH = pl.DeviceIdType.MESH


def lattice():
    axis_part = [(1, 0, 0), (-1, 0, 0), (0, 1, 0), (0, -1, 0), (0, 0, 1), (0, 0, -1)]
    edge_part = [
        (1, 1, 0),
        (-1, -1, 0),
        (1, -1, 0),
        (-1, 1, 0),
        (1, 0, 1),
        (-1, 0, -1),
        (1, 0, -1),
        (-1, 0, 1),
        (0, 1, 1),
        (0, -1, -1),
        (0, 1, -1),
        (0, -1, 1),
    ]
    vectors = np.array([(0, 0, 0)] + axis_part + edge_part) * 1.0
    weights = np.array([1.0 / 3.0] + [1.0 / 18.0] * 6 + [1.0 / 36.0] * 12)
    opposite = np.array(
        [int(np.argmin(np.abs(vectors + vectors[column]).sum(1))) for column in range(19)]
    )
    return (vectors, weights, opposite)


def orthonormal(monomials, weights):
    rows = []
    for entry in monomials:
        vector = entry * 1.0
        for sweep in range(2):
            for other in rows:
                vector = vector - np.sum(weights * vector * other) * other
        vector = vector / np.sqrt(np.sum(weights * vector * vector))
        rows.append(vector)
    return np.stack(rows, 0)


def basis_table():
    vectors, weights, opposite = lattice()
    x, y, z = (vectors[:, 0], vectors[:, 1], vectors[:, 2])
    monomials = [np.ones(19), x, y, z, x * x, y * y, z * z, x * y, x * z, y * z]
    monomials += [x * y * y, x * z * z, y * x * x, y * z * z, z * x * x, z * y * y]
    monomials += [x * x * y * y, x * x * z * z, y * y * z * z]
    return orthonormal(monomials, weights)


VECTORS, WEIGHTS, OPPOSITE = lattice()
BASIS = basis_table()
VEC = [tuple(int(c) for c in row) for row in VECTORS]
INDEX = {vec: i for i, vec in enumerate(VEC)}
OPP = [int(i) for i in OPPOSITE]
PUSH = [float(p) for p in 3.0 * WEIGHTS * VECTORS[:, 0]]


def moving(axis, sign):
    return [i for i in range(19) if VEC[i][axis] == sign]


def total(values):
    values = list(values)
    while len(values) > 1:
        pairs = [values[k] + values[k + 1] for k in range(0, len(values) - 1, 2)]
        values = pairs + values[len(values) - len(values) % 2 :]
    return values[0]


def weighted(coefs, values):
    return total([float(c) * v for c, v in zip(coefs, values) if abs(c) > 1e-9])


def density_of(f):
    return total(f)


def momentum_of(f, axis):
    return total(f[i] for i in moving(axis, 1)) - total(f[i] for i in moving(axis, -1))


def collide(*f):
    rho = density_of(f)
    mom = [momentum_of(f, a) for a in range(3)]
    inv = 1.0 / rho
    even = {0: f[0]}
    planes = [(0, 1), (0, 2), (1, 2)]
    unit = np.eye(3, dtype=int)
    diff, cross = {}, {}
    for a in range(3):
        p = INDEX[tuple(unit[a])]
        even[a + 1] = f[p] + f[OPP[p]]
        diff[(a,)] = f[p] - f[OPP[p]]
    for k, (a, b) in enumerate(planes):
        p, q = INDEX[tuple(unit[a] + unit[b])], INDEX[tuple(unit[a] - unit[b])]
        sp, sq = f[p] + f[OPP[p]], f[q] + f[OPP[q]]
        dp, dq = f[p] - f[OPP[p]], f[q] - f[OPP[q]]
        even[4 + k] = sp + sq
        cross[k] = sp - sq
        diff[(a, b)] = dp + dq
        diff[(b, a)] = dp - dq
    stress = []
    for a in range(3):
        near = [4 + k for k, pl_ in enumerate(planes) if a in pl_]
        second = even[a + 1] + even[near[0]] + even[near[1]]
        stress.append(second - rho * (1.0 / 3.0) - mom[a] * mom[a] * inv)
    for k, (a, b) in enumerate(planes):
        stress.append(cross[k] - mom[a] * mom[b] * inv)
    square = total([p * p for p in stress[:3]]) + 2.0 * total([p * p for p in stress[3:]])
    tau = 0.5 * (
        TAU_ZERO
        + jnp.sqrt(TAU_ZERO * TAU_ZERO + 18.0 * SMAGORINSKY * jnp.sqrt(square + TINY) * inv)
    )
    rate = 1.0 / tau
    relaxed = [p * rate for p in stress]
    trace = (relaxed[0] + relaxed[1] + relaxed[2]) * (1.0 / 3.0)
    members = [0] + [INDEX[tuple(unit[a])] for a in range(3)]
    members += [INDEX[tuple(unit[a] + unit[b])] for a, b in planes]
    ghosts = [weighted(BASIS[r][members], [even[c] for c in range(7)]) for r in (16, 17, 18)]
    drop_even = []
    for c, m in enumerate(members):
        part = weighted([WEIGHTS[m] * GHOST_RATES[r - 10] * BASIS[r][m] for r in (16, 17, 18)], ghosts)
        if c == 0:
            aniso = -trace
        elif c < 4:
            aniso = relaxed[c - 1] - trace
        else:
            a, b = planes[c - 4]
            aniso = relaxed[a] + relaxed[b] - trace
        drop_even.append(part + float(4.5 * WEIGHTS[m]) * aniso)
    drop_odd = {}
    for a in range(3):
        others = [b for b in range(3) if b != a]
        kinds = [(a,)] + [(a, b) for b in others]
        reps = [INDEX[tuple(unit[a])]] + [INDEX[tuple(unit[a] + unit[b])] for b in others]
        rows = (10 + 2 * a, 11 + 2 * a)
        odd = [weighted(BASIS[r][reps], [diff[k] for k in kinds]) for r in rows]
        for kind, m in zip(kinds, reps):
            drop_odd[kind] = weighted([WEIGHTS[m] * GHOST_RATES[r - 10] * BASIS[r][m] for r in rows], odd)
    out = [None] * 19
    out[0] = f[0] - drop_even[0]
    for a in range(3):
        p = INDEX[tuple(unit[a])]
        out[p] = f[p] - (drop_even[a + 1] + drop_odd[(a,)])
        out[OPP[p]] = f[OPP[p]] - (drop_even[a + 1] - drop_odd[(a,)])
    for k, (a, b) in enumerate(planes):
        p, q = INDEX[tuple(unit[a] + unit[b])], INDEX[tuple(unit[a] - unit[b])]
        shear = 0.25 * relaxed[3 + k]
        plus, minus = drop_even[4 + k] + shear, drop_even[4 + k] - shear
        odd_p = drop_odd[(a, b)] + drop_odd[(b, a)]
        odd_q = drop_odd[(a, b)] - drop_odd[(b, a)]
        out[p] = f[p] - (plus + odd_p)
        out[OPP[p]] = f[OPP[p]] - (plus - odd_p)
        out[q] = f[q] - (minus + odd_q)
        out[OPP[q]] = f[OPP[q]] - (minus - odd_q)
    return tuple(out)


HALO = [((1, 0), 0, 2), ((-1, 0), 2, 2), ((0, 1), 4, 1), ((0, -1), 5, 1)]
HALO += [((1, 1), 6, 1), ((-1, -1), 7, 1), ((1, -1), 8, 1), ((-1, 1), 9, 1)]
CORNER = {shift: start for shift, start, count in HALO[4:]}
SLOTS = 10


def near_offsets(size, reach):
    return sorted({d % size for d in range(-reach, reach + 1)})


def kernel(nx, ny, checkpoint, cotangent, area, cell, grad, area_grad, field, flats, speeds, thrusts,
           rotors, spread, grads, halo_out, halo_in, part_out, part_in, sum_out, sum_a, sum_b,
           halo_sent, halo_got, part_sent, part_got, sum_sent, sum_got):
    ix, iy = lax.axis_index("gx"), lax.axis_index("gy")
    near = [(dx, dy) for dx in near_offsets(nx, 2) for dy in near_offsets(ny, 2) if (dx, dy) != (0, 0)]
    low = SUBCELLS
    group = [(a, b) for a in range(low) for b in range(ny) if (a, b) != (0, 0)]
    far = list(range(1, nx // low))

    def at(dx, dy):
        return (lax.rem(ix + dx % nx, nx), lax.rem(iy + dy % ny, ny))

    base = lax.rem(ix, low)

    def in_group(a, b):
        return (ix - base + lax.rem(base + a, low), lax.rem(iy + b, ny))

    def in_far(c):
        return (lax.rem(ix + low * c, nx), iy)

    targets = [at(*o) for o in near] + [in_group(*o) for o in group] + [in_far(c) for c in far]
    barrier = pltpu.get_barrier_semaphore()
    for target in targets:
        pl.semaphore_signal(barrier, inc=1, device_id=target, device_id_type=MESH)

    span = checkpoint.shape[2]
    rows = checkpoint.shape[1]
    half = span - LANES
    row = lax.broadcasted_iota(jnp.int32, (rows, span), 0)
    lane = lax.broadcasted_iota(jnp.int32, (rows, span), 1)
    z = lax.bitwise_and(lane, NZ - 1)
    first_z, last_z = z == 0, z == NZ - 1
    row_h = lax.broadcasted_iota(jnp.int32, (rows, LANES), 0)
    lane_h = lax.broadcasted_iota(jnp.int32, (rows, LANES), 1)
    slot_h = lax.shift_right_logical(lane_h, 4)

    def onehots(t):
        index = cell[t : t + 1, :]
        across = lax.shift_right_arithmetic(index, 8)
        along = lax.bitwise_and(index, 255)
        pick_x = lax.broadcasted_iota(jnp.int32, (rows, LANES), 0) == across
        pick_j = lax.broadcasted_iota(jnp.int32, (span, LANES), 0) == along
        return pick_x, jnp.where(pick_j, 1.0, 0.0)

    for t in range(NTURB):
        pick_x, pick_j = onehots(t)
        weight = jnp.where(pick_x, area[t : t + 1, :], 0.0)
        spread[t] = lax.dot_general(
            weight, pick_j, (((1,), (1,)), ((), ())),
            precision=lax.Precision.HIGHEST, preferred_element_type=jnp.float32)
        grads[t] = jnp.zeros((rows, span), jnp.float32)
    denom = jnp.broadcast_to(jnp.sum(area[...], axis=1, keepdims=True), (NTURB, LANES))

    pl.semaphore_wait(barrier, len(targets))

    def stream(f, e):
        for sign in (1, -1):
            edge = rows - 1 if sign == 1 else 0
            packed = jnp.zeros((rows, span), jnp.float32)
            for k, i in enumerate(moving(0, sign)):
                packed = jnp.where(row == k, pltpu.roll(f[i], (k - edge) % rows, 0), packed)
            start = 0 if sign == 1 else 2
            halo_out[e, start] = packed[:, :LANES]
            halo_out[e, start + 1] = packed[:, half:]
        for sign in (1, -1):
            packed = jnp.zeros((rows, LANES), jnp.float32)
            for k, i in enumerate(moving(1, sign)):
                side = f[i][:, half:] if sign == 1 else f[i][:, :LANES]
                origin = LANES - NZ if sign == 1 else 0
                shift = (NZ * k - origin) % LANES
                side = pltpu.roll(side, shift, 1) if shift else side
                packed = jnp.where(slot_h == k, side, packed)
            halo_out[e, 4 if sign == 1 else 5] = packed
        for (dx, dy), start in CORNER.items():
            value = f[INDEX[(dx, dy, 0)]]
            halo_out[e, start] = value[:, half:] if dy == 1 else value[:, :LANES]
        for (dx, dy), start, count in HALO:
            pltpu.make_async_remote_copy(
                src_ref=halo_out.at[e, pl.ds(start, count)],
                dst_ref=halo_in.at[e, pl.ds(start, count)],
                send_sem=halo_sent.at[e], recv_sem=halo_got.at[e],
                device_id=at(dx, dy), device_id_type=MESH).start()
        pltpu.make_async_copy(halo_in.at[e], halo_in.at[e], halo_got.at[e]).wait()
        out = []
        for i in range(19):
            dx, dy, dz = VEC[i]
            value = f[i]
            if dx:
                edge = rows - 1 if dx == 1 else 0
                k = moving(0, dx).index(i)
                start = 0 if dx == 1 else 2
                got = jnp.concatenate([halo_in[e, start], halo_in[e, start + 1]], axis=1)
                shift = (edge - k) % rows
                got = pltpu.roll(got, shift, 0) if shift else got
                value = jnp.where(row == edge, got, value)
            if dy:
                k = moving(1, dy).index(i)
                origin = LANES - NZ if dy == 1 else 0
                shift = (origin - NZ * k) % LANES
                got = halo_in[e, 4 if dy == 1 else 5]
                got = pltpu.roll(got, shift, 1) if shift else got
                if dx:
                    edge = rows - 1 if dx == 1 else 0
                    got = jnp.where(row_h == edge, halo_in[e, CORNER[(dx, dy)]], got)
                if dy == 1:
                    side = jnp.where(lane_h >= LANES - NZ, got, value[:, half:])
                    value = jnp.concatenate([value[:, :half], side], axis=1)
                else:
                    side = jnp.where(lane_h < NZ, got, value[:, :LANES])
                    value = jnp.concatenate([side, value[:, LANES:]], axis=1)
            if dx:
                value = pltpu.roll(value, dx % rows, 0)
            shift = (NZ * dy + dz) % span
            if shift:
                value = pltpu.roll(value, shift, 1)
            if dz:
                value = jnp.where(first_z if dz == 1 else last_z, f[OPP[i]], value)
            out.append(value)
        return out

    def send_partial(value, e):
        sums = []
        for t in range(NTURB):
            prod = spread[t] * value
            sums.append(jnp.sum(prod[:, :LANES] + prod[:, half:], axis=0, keepdims=True))
        top = jnp.sum(jnp.concatenate(sums[:8], axis=0), axis=1, keepdims=True)
        bottom = jnp.sum(jnp.concatenate(sums[8:], axis=0), axis=1, keepdims=True)
        part_out[e] = jnp.where(lane_h < LANES // 2, top, bottom)
        for k, (dx, dy) in enumerate(near):
            pltpu.make_async_remote_copy(
                src_ref=part_out.at[e], dst_ref=part_in.at[e, k],
                send_sem=part_sent.at[e], recv_sem=part_got.at[e],
                device_id=at(dx, dy), device_id_type=MESH).start()

    def take_partial(e):
        pltpu.make_async_copy(part_in.at[e], part_in.at[e], part_got.at[e]).wait()
        both = total([part_out[e]] + [part_in[e, k] for k in range(len(near))])
        turned = pltpu.roll(both, LANES // 2, 1)
        left = lane_h < LANES // 2
        sums = jnp.concatenate([jnp.where(left, both, turned), jnp.where(left, turned, both)], axis=0)
        return sums / denom

    def wide(value, t):
        return jnp.broadcast_to(value[t : t + 1, 0:1], (rows, span))

    for i in range(19):
        field[i] = checkpoint[i]

    def forward(s, carry):
        flat = stream([field[i] for i in range(19)], s)
        for i in range(19):
            flats[s, i] = flat[i]
        speed = momentum_of(flat, 0) / density_of(flat)
        speeds[s] = speed
        send_partial(speed, s)
        moved = collide(*flat)
        rotor = take_partial(s)
        rotors[s] = rotor
        pull = total([spread[t] * wide(rotor, t) for t in range(NTURB)])
        thrusts[s] = pull
        force = -THRUST * speed * pull
        for i in range(19):
            field[i] = moved[i] + PUSH[i] * force if PUSH[i] != 0.0 else moved[i]
        return carry

    lax.fori_loop(0, STEPS, forward, 0)

    for i in range(19):
        field[i] = cotangent[i]

    def backward(n, carry):
        s, e = STEPS - 1 - n, STEPS + n
        adjoint = [field[i] for i in range(19)]
        flat = [flats[s, i] for i in range(19)]
        speed, pull, rotor = speeds[s], thrusts[s], rotors[s]
        force_bar = weighted(PUSH, adjoint)
        load = -THRUST * force_bar * speed
        send_partial(load, e)
        unused, pullback = jax.vjp(collide, *flat)
        flat_bar = pullback(tuple(adjoint))
        numer_bar = take_partial(e)
        spread_bar = total([spread[t] * wide(numer_bar, t) for t in range(NTURB)])
        speed_bar = (spread_bar - THRUST * force_bar * pull) / density_of(flat)
        for t in range(NTURB):
            turn = wide(rotor, t)
            grads[t] += turn * load + wide(numer_bar, t) * (speed - turn)
        flat_bar = [flat_bar[i] + (float(VEC[i][0]) - speed) * speed_bar for i in range(19)]
        pushed = stream([flat_bar[OPP[i]] for i in range(19)], e)
        for i in range(19):
            field[OPP[i]] = pushed[i]
        return carry

    lax.fori_loop(0, STEPS, backward, 0)

    for i in range(19):
        grad[i] = field[i]

    lines = []
    for t in range(NTURB):
        pick_x, pick_j = onehots(t)
        found = jnp.dot(grads[t], pick_j, precision=lax.Precision.HIGHEST,
                        preferred_element_type=jnp.float32)
        lines.append(jnp.sum(jnp.where(pick_x, found, 0.0), axis=0, keepdims=True))
    sum_out[0] = jnp.concatenate(lines, axis=0)
    for k, (a, b) in enumerate(group):
        pltpu.make_async_remote_copy(
            src_ref=sum_out.at[0], dst_ref=sum_a.at[k], send_sem=sum_sent.at[0],
            recv_sem=sum_got.at[0], device_id=in_group(a, b), device_id_type=MESH).start()
    pltpu.make_async_copy(sum_a, sum_a, sum_got.at[0]).wait()
    sum_out[1] = total([sum_out[0]] + [sum_a[k] for k in range(len(group))])
    for k, c in enumerate(far):
        pltpu.make_async_remote_copy(
            src_ref=sum_out.at[1], dst_ref=sum_b.at[k], send_sem=sum_sent.at[1],
            recv_sem=sum_got.at[1], device_id=in_far(c), device_id_type=MESH).start()
    pltpu.make_async_copy(sum_b, sum_b, sum_got.at[1]).wait()
    area_grad[...] = total([sum_out[1]] + [sum_b[k] for k in range(len(far))])

    for e in range(2 * STEPS):
        pltpu.make_async_copy(halo_in.at[e], halo_in.at[e], halo_sent.at[e]).wait()
        pltpu.make_async_copy(part_in.at[e], part_in.at[e], part_sent.at[e]).wait()
    pltpu.make_async_copy(sum_a, sum_a, sum_sent.at[0]).wait()
    pltpu.make_async_copy(sum_b, sum_b, sum_sent.at[1]).wait()


def body(checkpoint, cotangent, blade_area, hub_tile, point_side, point_local):
    nx, ny = lax.axis_size("gx"), lax.axis_size("gy")
    ix, iy = lax.axis_index("gx"), lax.axis_index("gy")
    pops, rows, span = checkpoint.shape
    side = point_side.reshape(NTURB, PTS)
    tile_x = (hub_tile[:, None] // ny + side // 3 - 1) % nx
    tile_y = (hub_tile[:, None] % ny + side % 3 - 1) % ny
    mine = (tile_x == ix) & (tile_y == iy)
    cell = jnp.where(mine, point_local.reshape(NTURB, PTS), -1)
    pad = ((0, 0), (0, LANES - PTS))
    cell = jnp.pad(cell, pad, constant_values=-1)
    area = jnp.pad(blade_area.reshape(NTURB, PTS), pad)
    near = len(near_offsets(nx, 2)) * len(near_offsets(ny, 2)) - 1
    group, far = SUBCELLS * ny - 1, nx // SUBCELLS - 1
    f32, dma = jnp.float32, pltpu.SemaphoreType.DMA
    tile = (rows, span)
    shapes = [(pops,) + tile, (STEPS, pops) + tile, (STEPS,) + tile, (STEPS,) + tile]
    shapes += [(STEPS, NTURB, LANES), (NTURB,) + tile, (NTURB,) + tile]
    shapes += [(2 * STEPS, SLOTS, rows, LANES)] * 2
    shapes += [(2 * STEPS, rows, LANES), (2 * STEPS, near, rows, LANES)]
    shapes += [(2, NTURB, LANES), (group, NTURB, LANES), (far, NTURB, LANES)]
    whole = pl.BlockSpec(memory_space=pltpu.VMEM)
    adjoint, grads = pl.pallas_call(
        functools.partial(kernel, nx, ny),
        out_shape=(jax.ShapeDtypeStruct(checkpoint.shape, f32),
                   jax.ShapeDtypeStruct((NTURB, LANES), f32)),
        in_specs=[whole] * 4,
        out_specs=(whole, whole),
        scratch_shapes=[pltpu.VMEM(shape, f32) for shape in shapes]
        + [dma((2 * STEPS,))] * 4 + [dma((2,))] * 2,
        compiler_params=pltpu.CompilerParams(
            collective_id=0, has_side_effects=True, vmem_limit_bytes=32 * 1024 * 1024),
    )(checkpoint, cotangent, area, cell)
    return adjoint, grads[:, :PTS].reshape(NTURB * PTS)


def solution(mesh):
    return jax.shard_map(
        body,
        mesh=mesh,
        in_specs=(P(None, "gx", "gy"), P(None, "gx", "gy"), P(), P(), P(), P()),
        out_specs=(P(None, "gx", "gy"), P()),
        check_vma=False,
    )
```

```python
import functools

import jax
import jax.numpy as jnp
import numpy as np
from jax import lax
from jax.experimental import pallas as pl
from jax.experimental.pallas import tpu as pltpu
from jax.sharding import PartitionSpec as P

NZ = 16
STEPS = 4
NTURB = 16
PTS = 96
LANES = 128
SUBCELLS = 4

TAU_ZERO = 0.52
SMAGORINSKY = 0.17 * 0.17
TINY = 1e-10
THRUST = 4.0
GHOST_RATES = np.array([1.05, 1.15, 1.25, 1.35, 1.45, 1.55, 1.65, 1.75, 1.85])
MESH = pl.DeviceIdType.MESH


def lattice():
    axis_part = [(1, 0, 0), (-1, 0, 0), (0, 1, 0), (0, -1, 0), (0, 0, 1), (0, 0, -1)]
    edge_part = [
        (1, 1, 0),
        (-1, -1, 0),
        (1, -1, 0),
        (-1, 1, 0),
        (1, 0, 1),
        (-1, 0, -1),
        (1, 0, -1),
        (-1, 0, 1),
        (0, 1, 1),
        (0, -1, -1),
        (0, 1, -1),
        (0, -1, 1),
    ]
    vectors = np.array([(0, 0, 0)] + axis_part + edge_part) * 1.0
    weights = np.array([1.0 / 3.0] + [1.0 / 18.0] * 6 + [1.0 / 36.0] * 12)
    opposite = np.array(
        [int(np.argmin(np.abs(vectors + vectors[column]).sum(1))) for column in range(19)]
    )
    return (vectors, weights, opposite)


def orthonormal(monomials, weights):
    rows = []
    for entry in monomials:
        vector = entry * 1.0
        for sweep in range(2):
            for other in rows:
                vector = vector - np.sum(weights * vector * other) * other
        vector = vector / np.sqrt(np.sum(weights * vector * vector))
        rows.append(vector)
    return np.stack(rows, 0)


def basis_table():
    vectors, weights, opposite = lattice()
    x, y, z = (vectors[:, 0], vectors[:, 1], vectors[:, 2])
    monomials = [np.ones(19), x, y, z, x * x, y * y, z * z, x * y, x * z, y * z]
    monomials += [x * y * y, x * z * z, y * x * x, y * z * z, z * x * x, z * y * y]
    monomials += [x * x * y * y, x * x * z * z, y * y * z * z]
    return orthonormal(monomials, weights)


VECTORS, WEIGHTS, OPPOSITE = lattice()
BASIS = basis_table()
VEC = [tuple(int(c) for c in row) for row in VECTORS]
INDEX = {vec: i for i, vec in enumerate(VEC)}
OPP = [int(i) for i in OPPOSITE]
PUSH = [float(p) for p in 3.0 * WEIGHTS * VECTORS[:, 0]]


def moving(axis, sign):
    return [i for i in range(19) if VEC[i][axis] == sign]


def total(values):
    values = list(values)
    while len(values) > 1:
        pairs = [values[k] + values[k + 1] for k in range(0, len(values) - 1, 2)]
        values = pairs + values[len(values) - len(values) % 2 :]
    return values[0]


def weighted(coefs, values):
    return total([float(c) * v for c, v in zip(coefs, values) if abs(c) > 1e-9])


def density_of(f):
    return total(f)


def momentum_of(f, axis):
    return total(f[i] for i in moving(axis, 1)) - total(f[i] for i in moving(axis, -1))


def collide(*f):
    rho = density_of(f)
    mom = [momentum_of(f, a) for a in range(3)]
    inv = 1.0 / rho
    even = {0: f[0]}
    planes = [(0, 1), (0, 2), (1, 2)]
    unit = np.eye(3, dtype=int)
    diff, cross = {}, {}
    for a in range(3):
        p = INDEX[tuple(unit[a])]
        even[a + 1] = f[p] + f[OPP[p]]
        diff[(a,)] = f[p] - f[OPP[p]]
    for k, (a, b) in enumerate(planes):
        p, q = INDEX[tuple(unit[a] + unit[b])], INDEX[tuple(unit[a] - unit[b])]
        sp, sq = f[p] + f[OPP[p]], f[q] + f[OPP[q]]
        dp, dq = f[p] - f[OPP[p]], f[q] - f[OPP[q]]
        even[4 + k] = sp + sq
        cross[k] = sp - sq
        diff[(a, b)] = dp + dq
        diff[(b, a)] = dp - dq
    stress = []
    for a in range(3):
        near = [4 + k for k, pl_ in enumerate(planes) if a in pl_]
        second = even[a + 1] + even[near[0]] + even[near[1]]
        stress.append(second - rho * (1.0 / 3.0) - mom[a] * mom[a] * inv)
    for k, (a, b) in enumerate(planes):
        stress.append(cross[k] - mom[a] * mom[b] * inv)
    square = total([p * p for p in stress[:3]]) + 2.0 * total([p * p for p in stress[3:]])
    tau = 0.5 * (
        TAU_ZERO
        + jnp.sqrt(TAU_ZERO * TAU_ZERO + 18.0 * SMAGORINSKY * jnp.sqrt(square + TINY) * inv)
    )
    rate = 1.0 / tau
    relaxed = [p * rate for p in stress]
    trace = (relaxed[0] + relaxed[1] + relaxed[2]) * (1.0 / 3.0)
    members = [0] + [INDEX[tuple(unit[a])] for a in range(3)]
    members += [INDEX[tuple(unit[a] + unit[b])] for a, b in planes]
    ghosts = [weighted(BASIS[r][members], [even[c] for c in range(7)]) for r in (16, 17, 18)]
    drop_even = []
    for c, m in enumerate(members):
        part = weighted([WEIGHTS[m] * GHOST_RATES[r - 10] * BASIS[r][m] for r in (16, 17, 18)], ghosts)
        if c == 0:
            aniso = -trace
        elif c < 4:
            aniso = relaxed[c - 1] - trace
        else:
            a, b = planes[c - 4]
            aniso = relaxed[a] + relaxed[b] - trace
        drop_even.append(part + float(4.5 * WEIGHTS[m]) * aniso)
    drop_odd = {}
    for a in range(3):
        others = [b for b in range(3) if b != a]
        kinds = [(a,)] + [(a, b) for b in others]
        reps = [INDEX[tuple(unit[a])]] + [INDEX[tuple(unit[a] + unit[b])] for b in others]
        rows = (10 + 2 * a, 11 + 2 * a)
        odd = [weighted(BASIS[r][reps], [diff[k] for k in kinds]) for r in rows]
        for kind, m in zip(kinds, reps):
            drop_odd[kind] = weighted([WEIGHTS[m] * GHOST_RATES[r - 10] * BASIS[r][m] for r in rows], odd)
    out = [None] * 19
    out[0] = f[0] - drop_even[0]
    for a in range(3):
        p = INDEX[tuple(unit[a])]
        out[p] = f[p] - (drop_even[a + 1] + drop_odd[(a,)])
        out[OPP[p]] = f[OPP[p]] - (drop_even[a + 1] - drop_odd[(a,)])
    for k, (a, b) in enumerate(planes):
        p, q = INDEX[tuple(unit[a] + unit[b])], INDEX[tuple(unit[a] - unit[b])]
        shear = 0.25 * relaxed[3 + k]
        plus, minus = drop_even[4 + k] + shear, drop_even[4 + k] - shear
        odd_p = drop_odd[(a, b)] + drop_odd[(b, a)]
        odd_q = drop_odd[(a, b)] - drop_odd[(b, a)]
        out[p] = f[p] - (plus + odd_p)
        out[OPP[p]] = f[OPP[p]] - (plus - odd_p)
        out[q] = f[q] - (minus + odd_q)
        out[OPP[q]] = f[OPP[q]] - (minus - odd_q)
    return tuple(out)


RIMS = [(1, 0, 0, 0, 2), (-1, 0, 2, 2, 2), (0, 1, 4, 4, 1), (0, -1, 5, 5, 1)]
RIMS += [(1, 1, 4, 6, 1), (1, -1, 5, 7, 1), (-1, 1, 4, 8, 1), (-1, -1, 5, 9, 1)]
CORNER = {(dx, dy): dst for dx, dy, src, dst, count in RIMS[4:]}
SIDES = [(dx, dy) for dy in (1, -1) for dx in (0, 1, -1)]
REACH = 3
HALOS = 2 * STEPS
PARTIALS = 2 * STEPS - 1


def near_offsets(size, reach):
    return sorted({d % size for d in range(-reach, reach + 1)})


def rim_copies(nx, ny):
    copies = []
    for dx, dy, src, dst, count in RIMS:
        where = (dx % nx, dy % ny)
        if copies:
            last, s, d, c = copies[-1]
            if last == where and s + c == src and d + c == dst:
                copies[-1] = (last, s, d, c + count)
                continue
        copies.append((where, src, dst, count))
    return copies


def thirds(value):
    high = value.astype(jnp.bfloat16).astype(jnp.float32)
    rest = value - high
    middle = rest.astype(jnp.bfloat16).astype(jnp.float32)
    parts = [high, middle, rest - middle, jnp.zeros_like(value)]
    return jnp.concatenate(parts, axis=0).astype(jnp.bfloat16)


def join_thirds(product):
    rows = product.shape[0] // 4
    return product[:rows] + (product[rows : 2 * rows] + product[2 * rows : 3 * rows])


def kernel(nx, ny, checkpoint, cotangent, area, cell, grad, area_grad, flats, thrusts, spread, grads,
           rim_y, halo_out, halo_in, rim_out, rim_in, part_out, part_in, sum_out, sum_a, sum_b,
           halo_sent, halo_got, rim_sent, rim_got, part_sent, part_got, sum_sent, sum_got):
    ix, iy = lax.axis_index("gx"), lax.axis_index("gy")
    near = [(dx, dy) for dx in near_offsets(nx, REACH) for dy in near_offsets(ny, REACH)]
    near = [o for o in near if o != (0, 0)]
    low = SUBCELLS
    group = [(a, b) for a in range(low) for b in range(ny) if (a, b) != (0, 0)]
    far = list(range(1, nx // low))

    def at(dx, dy):
        return (lax.rem(ix + dx, nx), lax.rem(iy + dy, ny))

    base = lax.rem(ix, low)

    def in_group(a, b):
        return (ix - base + lax.rem(base + a, low), lax.rem(iy + b, ny))

    def in_far(c):
        return (lax.rem(ix + low * c, nx), iy)

    targets = [at(*o) for o in near] + [in_group(*o) for o in group] + [in_far(c) for c in far]
    barrier = pltpu.get_barrier_semaphore()
    for target in targets:
        pl.semaphore_signal(barrier, inc=1, device_id=target, device_id_type=MESH)

    rows, span = checkpoint.shape[1:]
    half = span - LANES
    row = lax.broadcasted_iota(jnp.int32, (rows, span), 0)
    lane = lax.broadcasted_iota(jnp.int32, (rows, span), 1)
    z = lax.bitwise_and(lane, NZ - 1)
    first_z, last_z = z == 0, z == NZ - 1
    row_h = lax.broadcasted_iota(jnp.int32, (rows, LANES), 0)
    lane_h = lax.broadcasted_iota(jnp.int32, (rows, LANES), 1)
    slot_h = lax.shift_right_logical(lane_h, 4)
    row_t = lax.broadcasted_iota(jnp.int32, (NTURB, LANES), 0)
    lane_t = lax.broadcasted_iota(jnp.int32, (NTURB, LANES), 1)

    def turned(value, shift, axis):
        shift = shift % value.shape[axis]
        return pltpu.roll(value, shift, axis) if shift else value

    def edge_of(sign):
        return rows - 1 if sign == 1 else 0

    def rim_lane(sign):
        return LANES - NZ if sign == 1 else 0

    def side_of(value, sign):
        return value[:, half:] if sign == 1 else value[:, :LANES]

    def pack_x(values, sign):
        packed = jnp.zeros((rows, span), jnp.float32)
        for k, value in enumerate(values):
            packed = jnp.where(row == k, turned(value, k - edge_of(sign), 0), packed)
        return packed

    def pack_y(values, sign):
        packed = jnp.zeros((rows, LANES), jnp.float32)
        for k, value in enumerate(values):
            moved = turned(side_of(value, sign), NZ * k - rim_lane(sign), 1)
            packed = jnp.where(slot_h == k, moved, packed)
        return packed

    def send_halo(f, fields, e):
        for sign, start in ((1, 0), (-1, 2)):
            packed = pack_x([f[i] for i in moving(0, sign)] + fields, sign)
            halo_out[e, start] = packed[:, :LANES]
            halo_out[e, start + 1] = packed[:, half:]
        for sign, start in ((1, 4), (-1, 5)):
            halo_out[e, start] = pack_y([f[i] for i in moving(1, sign)] + fields, sign)
        for where, src, dst, count in rim_copies(nx, ny):
            pltpu.make_async_remote_copy(
                src_ref=halo_out.at[e, pl.ds(src, count)],
                dst_ref=halo_in.at[e, pl.ds(dst, count)],
                send_sem=halo_sent.at[e], recv_sem=halo_got.at[e],
                device_id=at(*where), device_id_type=MESH).start()

    def lane_blocks(value):
        out = []
        for h in range(2):
            picked = jnp.where(lax.shift_right_logical(lane_t, 4) + 8 * h == row_t, value, 0.0)
            line = jnp.sum(picked, axis=0, keepdims=True)
            out.append(jnp.broadcast_to(line, (rows, LANES)))
        return out

    def pulls_x(sign, rates):
        start = 0 if sign == 1 else 4
        out = []
        for rate in rates:
            halves = []
            for c in range(2):
                both = rim_in[start + c] * rate[:8] + rim_in[start + 2 + c] * rate[8:]
                halves.append(jnp.sum(both, axis=0, keepdims=True))
            out.append(jnp.concatenate(halves, axis=1))
        return out

    def pulls_y(side, blocks):
        out = []
        for pair in blocks:
            both = rim_y[side, 0] * pair[0] + rim_y[side, 1] * pair[1]
            for shift in (16, 32, 64):
                both = both + pltpu.roll(both, shift, 1)
            out.append(both)
        return out

    def stream(f, e, count=0, rates=(), correct=None):
        pltpu.make_async_copy(halo_in.at[e], halo_in.at[e], halo_got.at[e]).wait()
        blocks = [lane_blocks(rate) for rate in rates]
        from_x, from_y = {}, {}
        for sign, start in ((1, 0), (-1, 2)):
            got = jnp.concatenate([halo_in[e, start], halo_in[e, start + 1]], axis=1)
            add = None
            if correct is not None:
                fields = [turned(got, edge_of(sign) - 5 - k, 0) for k in range(count)]
                add = correct(fields, pulls_x(sign, rates))
            for k, i in enumerate(moving(0, sign)):
                value = turned(got, edge_of(sign) - k, 0)
                from_x[i] = value if add is None else value + add(i)
        for side, (dx, dy) in enumerate(SIDES):
            got = halo_in[e, 4 if dy == 1 else 5]
            if dx:
                got = jnp.where(row_h == edge_of(dx), halo_in[e, CORNER[(dx, dy)]], got)
            add = None
            if correct is not None and (dx or count > 1):
                fields = [turned(got, rim_lane(dy) - NZ * (5 + k), 1) for k in range(count)]
                add = correct(fields, pulls_y(side, blocks))
            for k, i in enumerate(moving(1, dy)):
                if VEC[i][0] == dx:
                    value = turned(got, rim_lane(dy) - NZ * k, 1)
                    from_y[i] = value if add is None else value + add(i)
        out = []
        for i in range(19):
            dx, dy, dz = VEC[i]
            value = f[i]
            if dx:
                value = jnp.where(row == edge_of(dx), from_x[i], value)
            if dy == 1:
                edge = jnp.where(lane_h >= LANES - NZ, from_y[i], value[:, half:])
                value = jnp.concatenate([value[:, :half], edge], axis=1)
            elif dy == -1:
                edge = jnp.where(lane_h < NZ, from_y[i], value[:, :LANES])
                value = jnp.concatenate([edge, value[:, LANES:]], axis=1)
            value = turned(turned(value, dx, 0), NZ * dy + dz, 1)
            if dz:
                value = jnp.where(first_z if dz == 1 else last_z, f[OPP[i]], value)
            out.append(value)
        return out

    def turbine_sums(value):
        sums = []
        for t in range(NTURB):
            prod = spread[t] * value
            sums.append(jnp.sum(prod[:, :LANES] + prod[:, half:], axis=0, keepdims=True))
        sums = jnp.sum(jnp.concatenate(sums, axis=0), axis=1, keepdims=True)
        return jnp.broadcast_to(sums, (NTURB, LANES))

    def send_partials(sums, e):
        width = LANES // (2 * len(sums))
        packed = sums[-1][8:]
        pieces = [s[h : h + 8] for s in sums for h in (0, 8)]
        for k in range(len(pieces) - 2, -1, -1):
            packed = jnp.where(lane_h < width * (k + 1), pieces[k], packed)
        part_out[e] = packed
        for k, (dx, dy) in enumerate(near):
            pltpu.make_async_remote_copy(
                src_ref=part_out.at[e], dst_ref=part_in.at[e, k],
                send_sem=part_sent.at[e], recv_sem=part_got.at[e],
                device_id=at(dx, dy), device_id_type=MESH).start()

    def take_partials(count, e):
        width = LANES // (2 * count)
        pltpu.make_async_copy(part_in.at[e], part_in.at[e], part_got.at[e]).wait()
        both = total([part_out[e]] + [part_in[e, k] for k in range(len(near))])
        pieces = []
        for k in range(2 * count):
            inside = (lane_h >= width * k) & (lane_h < width * (k + 1))
            piece, shift = jnp.where(inside, both, 0.0), width
            while shift < LANES:
                piece, shift = piece + pltpu.roll(piece, shift, 1), 2 * shift
            pieces.append(piece)
        return [jnp.concatenate(pieces[2 * k : 2 * k + 2], axis=0) / denom for k in range(count)]

    def wide(value, t):
        line = jnp.broadcast_to(value[t : t + 1], (rows, LANES))
        return jnp.concatenate([line] * (span // LANES), axis=1)

    def pull_of(rate):
        return total([spread[t] * wide(rate, t) for t in range(NTURB)])

    def onehots(t):
        index = cell[t : t + 1, :]
        across = lax.shift_right_arithmetic(index, 8)
        along = lax.bitwise_and(index, 255)
        pick_x = lax.broadcasted_iota(jnp.int32, (rows, LANES), 0) == across
        pick_j = lax.broadcasted_iota(jnp.int32, (span, LANES), 0) == along
        return pick_x, jnp.where(pick_j, 1.0, 0.0).astype(jnp.bfloat16)

    def at_points(fields):
        lines = []
        for t in range(NTURB):
            pick_x, pick_j = onehots(t)
            found = join_thirds(jnp.dot(thirds(fields(t)), pick_j, preferred_element_type=jnp.float32))
            lines.append(jnp.sum(jnp.where(pick_x, found, 0.0), axis=0, keepdims=True))
        return jnp.concatenate(lines, axis=0)

    def sum_first(value, r):
        sum_out[r, 0] = value
        for k, (a, b) in enumerate(group):
            pltpu.make_async_remote_copy(
                src_ref=sum_out.at[r, 0], dst_ref=sum_a.at[r, k], send_sem=sum_sent.at[2 * r],
                recv_sem=sum_got.at[2 * r], device_id=in_group(a, b), device_id_type=MESH).start()

    def sum_second(r):
        pltpu.make_async_copy(sum_a.at[r], sum_a.at[r], sum_got.at[2 * r]).wait()
        sum_out[r, 1] = total([sum_out[r, 0]] + [sum_a[r, k] for k in range(len(group))])
        for k, c in enumerate(far):
            pltpu.make_async_remote_copy(
                src_ref=sum_out.at[r, 1], dst_ref=sum_b.at[r, k], send_sem=sum_sent.at[2 * r + 1],
                recv_sem=sum_got.at[2 * r + 1], device_id=in_far(c), device_id_type=MESH).start()

    def sum_last(r):
        pltpu.make_async_copy(sum_b.at[r], sum_b.at[r], sum_got.at[2 * r + 1]).wait()
        return total([sum_out[r, 1]] + [sum_b[r, k] for k in range(len(far))])

    field = [checkpoint[i] for i in range(19)]
    pl.semaphore_wait(barrier, len(targets))
    send_halo(field, [], 0)

    for t in range(NTURB):
        pick_x, pick_j = onehots(t)
        weight = jnp.where(pick_x, area[t : t + 1, :], 0.0)
        spread[t] = join_thirds(lax.dot_general(
            thirds(weight), pick_j, (((1,), (1,)), ((), ())), preferred_element_type=jnp.float32))
    denom = jnp.broadcast_to(jnp.sum(area[...], axis=1, keepdims=True), (NTURB, LANES))
    for h in range(2):
        mine = [spread[8 * h + k] for k in range(8)]
        for sign, start in ((1, 0), (-1, 4)):
            packed = pack_x(mine, sign)
            rim_out[start + 2 * h] = packed[:, :LANES]
            rim_out[start + 2 * h + 1] = packed[:, half:]
        for sign, start in ((1, 8), (-1, 10)):
            rim_out[start + h] = pack_y(mine, sign)
    for where, src, dst, count in rim_copies(nx, ny):
        pltpu.make_async_remote_copy(
            src_ref=rim_out.at[pl.ds(2 * src, 2 * count)],
            dst_ref=rim_in.at[pl.ds(2 * dst, 2 * count)],
            send_sem=rim_sent.at[0], recv_sem=rim_got.at[0],
            device_id=at(*where), device_id_type=MESH).start()

    def forced(fields, pulls):
        force = -THRUST * fields[0] * pulls[0]
        return lambda i: PUSH[i] * force

    def speed_fixed(fields, pulls):
        speed_bar = fields[1] * pulls[0] + fields[2] * pulls[1]
        parts = {c: (float(-c) - fields[0]) * speed_bar for c in (-1, 0, 1)}
        return lambda i: parts[VEC[i][0]]

    rotors, speeds = [], []
    flat = stream(field, 0)
    for s in range(STEPS):
        for i in range(19):
            flats[s, i] = flat[i]
        speed = momentum_of(flat, 0) / density_of(flat)
        speeds.append(speed)
        if s == STEPS - 1:
            break
        send_partials([turbine_sums(speed)], s)
        moved = collide(*flat)
        send_halo(moved, [speed], s + 1)
        if s == 0:
            pltpu.make_async_copy(rim_in, rim_in, rim_got.at[0]).wait()
            for side, (dx, dy) in enumerate(SIDES):
                for h in range(2):
                    value = rim_in[(8 if dy == 1 else 10) + h]
                    if dx:
                        corner = rim_in[2 * CORNER[(dx, dy)] + h]
                        value = jnp.where(row_h == edge_of(dx), corner, value)
                    rim_y[side, h] = value
        rotor = take_partials(1, s)[0]
        rotors.append(rotor)
        pull = pull_of(rotor)
        thrusts[s] = pull
        add = forced([speed], [pull])
        field = [moved[i] + add(i) if PUSH[i] != 0.0 else moved[i] for i in range(19)]
        flat = stream(field, s + 1, 1, [rotor], forced)

    adjoint = [cotangent[i] for i in range(19)]
    for n in range(STEPS):
        s, e = STEPS - 1 - n, STEPS + n
        flat = [flats[s, i] for i in range(19)]
        speed = speeds[s]
        force_bar = weighted(PUSH, adjoint)
        load = -THRUST * force_bar * speed
        load_sums = turbine_sums(load)
        if n == 0:
            send_partials([turbine_sums(speed), load_sums], s)
        else:
            send_partials([load_sums], s + 2 * n)
        if n == STEPS - 1:
            rotor = rotors[s]
            found = at_points(lambda t: grads[t] + wide(rotor, t) * load)
            sum_first(jnp.where(lane_t < PTS, found, load_sums), 1)
        unused, pullback = jax.vjp(collide, *flat)
        flat_bar = pullback(tuple(adjoint))
        inverse = 1.0 / density_of(flat)
        fields = [speed, inverse, -THRUST * force_bar * inverse]
        turned_bar = [flat_bar[OPP[i]] for i in range(19)]
        send_halo(turned_bar, fields, e)
        if n == 0:
            first = at_points(lambda t: speeds[0] - wide(rotors[0], t))
            sum_first(first, 0)
            rotor, numer_bar = take_partials(2, s)
            pull = pull_of(rotor)
        else:
            if n == 1:
                sum_second(0)
            if n == STEPS - 1:
                sum_second(1)
            rotor, pull = rotors[s], thrusts[s]
            numer_bar = take_partials(1, s + 2 * n)[0]
        add = speed_fixed(fields, [pull_of(numer_bar), pull])
        field = [turned_bar[i] + add(i) for i in range(19)]
        pushed = stream(field, e, 3, [numer_bar, rotor], speed_fixed)
        adjoint = [pushed[OPP[i]] for i in range(19)]
        if n < STEPS - 1:
            for t in range(NTURB):
                turn = wide(rotor, t)
                part = turn * load + wide(numer_bar, t) * (speed - turn)
                grads[t] = part if n == 0 else grads[t] + part

    for i in range(19):
        grad[i] = adjoint[i]
    spread_of = sum_last(0)
    sums = sum_last(1)
    numer_bar = jnp.broadcast_to(sums[:, PTS : PTS + 1], (NTURB, LANES)) / denom
    area_grad[...] = sums + numer_bar * spread_of

    for e in range(HALOS):
        pltpu.make_async_copy(halo_in.at[e], halo_in.at[e], halo_sent.at[e]).wait()
    for e in range(PARTIALS):
        pltpu.make_async_copy(part_in.at[e], part_in.at[e], part_sent.at[e]).wait()
    pltpu.make_async_copy(rim_in, rim_in, rim_sent.at[0]).wait()
    for r in range(2):
        pltpu.make_async_copy(sum_a.at[r], sum_a.at[r], sum_sent.at[2 * r]).wait()
        pltpu.make_async_copy(sum_b.at[r], sum_b.at[r], sum_sent.at[2 * r + 1]).wait()


def body(checkpoint, cotangent, blade_area, hub_tile, point_side, point_local):
    nx, ny = lax.axis_size("gx"), lax.axis_size("gy")
    ix, iy = lax.axis_index("gx"), lax.axis_index("gy")
    pops, rows, span = checkpoint.shape
    side = point_side.reshape(NTURB, PTS)
    tile_x = (hub_tile[:, None] // ny + side // 3 - 1) % nx
    tile_y = (hub_tile[:, None] % ny + side % 3 - 1) % ny
    mine = (tile_x == ix) & (tile_y == iy)
    cell = jnp.where(mine, point_local.reshape(NTURB, PTS), -1)
    pad = ((0, 0), (0, LANES - PTS))
    cell = jnp.pad(cell, pad, constant_values=-1)
    area = jnp.pad(blade_area.reshape(NTURB, PTS), pad)
    near = len(near_offsets(nx, REACH)) * len(near_offsets(ny, REACH)) - 1
    group, far = SUBCELLS * ny - 1, nx // SUBCELLS - 1
    f32, dma = jnp.float32, pltpu.SemaphoreType.DMA
    tile, vreg = (rows, span), (rows, LANES)
    shapes = [(STEPS, pops) + tile, (STEPS,) + tile, (NTURB,) + tile, (NTURB,) + tile]
    shapes += [(6, 2) + vreg, (HALOS, 6) + vreg, (HALOS, 10) + vreg, (12,) + vreg, (20,) + vreg]
    shapes += [(PARTIALS,) + vreg, (PARTIALS, near) + vreg]
    shapes += [(2, 2, NTURB, LANES), (2, group, NTURB, LANES), (2, far, NTURB, LANES)]
    whole = pl.BlockSpec(memory_space=pltpu.VMEM)
    adjoint, grads = pl.pallas_call(
        functools.partial(kernel, nx, ny),
        out_shape=(jax.ShapeDtypeStruct(checkpoint.shape, f32),
                   jax.ShapeDtypeStruct((NTURB, LANES), f32)),
        in_specs=[whole] * 4,
        out_specs=(whole, whole),
        scratch_shapes=[pltpu.VMEM(shape, f32) for shape in shapes]
        + [dma((HALOS,))] * 2 + [dma((1,))] * 2 + [dma((PARTIALS,))] * 2 + [dma((4,))] * 2,
        compiler_params=pltpu.CompilerParams(
            collective_id=0, has_side_effects=True, vmem_limit_bytes=32 * 1024 * 1024),
    )(checkpoint, cotangent, area, cell)
    return adjoint, grads[:, :PTS].reshape(NTURB * PTS)


def solution(mesh):
    return jax.shard_map(
        body,
        mesh=mesh,
        in_specs=(P(None, "gx", "gy"), P(None, "gx", "gy"), P(), P(), P(), P()),
        out_specs=(P(None, "gx", "gy"), P()),
        check_vma=False,
    )
```

```python
import functools

import jax
import jax.numpy as jnp
import numpy as np
from jax import lax
from jax.experimental import pallas as pl
from jax.experimental.pallas import tpu as pltpu
from jax.sharding import PartitionSpec as P

NZ = 16
STEPS = 4
NTURB = 16
PTS = 96
LANES = 128
SUBCELLS = 4

TAU_ZERO = 0.52
SMAGORINSKY = 0.17 * 0.17
TINY = 1e-10
THRUST = 4.0
GHOST_RATES = np.array([1.05, 1.15, 1.25, 1.35, 1.45, 1.55, 1.65, 1.75, 1.85])
MESH = pl.DeviceIdType.MESH


def lattice():
    axis_part = [(1, 0, 0), (-1, 0, 0), (0, 1, 0), (0, -1, 0), (0, 0, 1), (0, 0, -1)]
    edge_part = [
        (1, 1, 0),
        (-1, -1, 0),
        (1, -1, 0),
        (-1, 1, 0),
        (1, 0, 1),
        (-1, 0, -1),
        (1, 0, -1),
        (-1, 0, 1),
        (0, 1, 1),
        (0, -1, -1),
        (0, 1, -1),
        (0, -1, 1),
    ]
    vectors = np.array([(0, 0, 0)] + axis_part + edge_part) * 1.0
    weights = np.array([1.0 / 3.0] + [1.0 / 18.0] * 6 + [1.0 / 36.0] * 12)
    opposite = np.array(
        [int(np.argmin(np.abs(vectors + vectors[column]).sum(1))) for column in range(19)]
    )
    return (vectors, weights, opposite)


def orthonormal(monomials, weights):
    rows = []
    for entry in monomials:
        vector = entry * 1.0
        for sweep in range(2):
            for other in rows:
                vector = vector - np.sum(weights * vector * other) * other
        vector = vector / np.sqrt(np.sum(weights * vector * vector))
        rows.append(vector)
    return np.stack(rows, 0)


def basis_table():
    vectors, weights, opposite = lattice()
    x, y, z = (vectors[:, 0], vectors[:, 1], vectors[:, 2])
    monomials = [np.ones(19), x, y, z, x * x, y * y, z * z, x * y, x * z, y * z]
    monomials += [x * y * y, x * z * z, y * x * x, y * z * z, z * x * x, z * y * y]
    monomials += [x * x * y * y, x * x * z * z, y * y * z * z]
    return orthonormal(monomials, weights)


VECTORS, WEIGHTS, OPPOSITE = lattice()
BASIS = basis_table()
VEC = [tuple(int(c) for c in row) for row in VECTORS]
INDEX = {vec: i for i, vec in enumerate(VEC)}
OPP = [int(i) for i in OPPOSITE]
PUSH = [float(p) for p in 3.0 * WEIGHTS * VECTORS[:, 0]]


def moving(axis, sign):
    return [i for i in range(19) if VEC[i][axis] == sign]


def total(values):
    values = list(values)
    while len(values) > 1:
        pairs = [values[k] + values[k + 1] for k in range(0, len(values) - 1, 2)]
        values = pairs + values[len(values) - len(values) % 2 :]
    return values[0]


def weighted(coefs, values):
    return total([float(c) * v for c, v in zip(coefs, values) if abs(c) > 1e-9])


def density_of(f):
    return total(f)


def momentum_of(f, axis):
    return total(f[i] for i in moving(axis, 1)) - total(f[i] for i in moving(axis, -1))


def collide(*f):
    rho = density_of(f)
    mom = [momentum_of(f, a) for a in range(3)]
    inv = 1.0 / rho
    even = {0: f[0]}
    planes = [(0, 1), (0, 2), (1, 2)]
    unit = np.eye(3, dtype=int)
    diff, cross = {}, {}
    for a in range(3):
        p = INDEX[tuple(unit[a])]
        even[a + 1] = f[p] + f[OPP[p]]
        diff[(a,)] = f[p] - f[OPP[p]]
    for k, (a, b) in enumerate(planes):
        p, q = INDEX[tuple(unit[a] + unit[b])], INDEX[tuple(unit[a] - unit[b])]
        sp, sq = f[p] + f[OPP[p]], f[q] + f[OPP[q]]
        dp, dq = f[p] - f[OPP[p]], f[q] - f[OPP[q]]
        even[4 + k] = sp + sq
        cross[k] = sp - sq
        diff[(a, b)] = dp + dq
        diff[(b, a)] = dp - dq
    stress = []
    for a in range(3):
        near = [4 + k for k, pl_ in enumerate(planes) if a in pl_]
        second = even[a + 1] + even[near[0]] + even[near[1]]
        stress.append(second - rho * (1.0 / 3.0) - mom[a] * mom[a] * inv)
    for k, (a, b) in enumerate(planes):
        stress.append(cross[k] - mom[a] * mom[b] * inv)
    square = total([p * p for p in stress[:3]]) + 2.0 * total([p * p for p in stress[3:]])
    tau = 0.5 * (
        TAU_ZERO
        + jnp.sqrt(TAU_ZERO * TAU_ZERO + 18.0 * SMAGORINSKY * jnp.sqrt(square + TINY) * inv)
    )
    rate = 1.0 / tau
    relaxed = [p * rate for p in stress]
    trace = (relaxed[0] + relaxed[1] + relaxed[2]) * (1.0 / 3.0)
    members = [0] + [INDEX[tuple(unit[a])] for a in range(3)]
    members += [INDEX[tuple(unit[a] + unit[b])] for a, b in planes]
    ghosts = [weighted(BASIS[r][members], [even[c] for c in range(7)]) for r in (16, 17, 18)]
    drop_even = []
    for c, m in enumerate(members):
        part = weighted([WEIGHTS[m] * GHOST_RATES[r - 10] * BASIS[r][m] for r in (16, 17, 18)], ghosts)
        if c == 0:
            aniso = -trace
        elif c < 4:
            aniso = relaxed[c - 1] - trace
        else:
            a, b = planes[c - 4]
            aniso = relaxed[a] + relaxed[b] - trace
        drop_even.append(part + float(4.5 * WEIGHTS[m]) * aniso)
    drop_odd = {}
    for a in range(3):
        others = [b for b in range(3) if b != a]
        kinds = [(a,)] + [(a, b) for b in others]
        reps = [INDEX[tuple(unit[a])]] + [INDEX[tuple(unit[a] + unit[b])] for b in others]
        rows = (10 + 2 * a, 11 + 2 * a)
        odd = [weighted(BASIS[r][reps], [diff[k] for k in kinds]) for r in rows]
        for kind, m in zip(kinds, reps):
            drop_odd[kind] = weighted([WEIGHTS[m] * GHOST_RATES[r - 10] * BASIS[r][m] for r in rows], odd)
    out = [None] * 19
    out[0] = f[0] - drop_even[0]
    for a in range(3):
        p = INDEX[tuple(unit[a])]
        out[p] = f[p] - (drop_even[a + 1] + drop_odd[(a,)])
        out[OPP[p]] = f[OPP[p]] - (drop_even[a + 1] - drop_odd[(a,)])
    for k, (a, b) in enumerate(planes):
        p, q = INDEX[tuple(unit[a] + unit[b])], INDEX[tuple(unit[a] - unit[b])]
        shear = 0.25 * relaxed[3 + k]
        plus, minus = drop_even[4 + k] + shear, drop_even[4 + k] - shear
        odd_p = drop_odd[(a, b)] + drop_odd[(b, a)]
        odd_q = drop_odd[(a, b)] - drop_odd[(b, a)]
        out[p] = f[p] - (plus + odd_p)
        out[OPP[p]] = f[OPP[p]] - (plus - odd_p)
        out[q] = f[q] - (minus + odd_q)
        out[OPP[q]] = f[OPP[q]] - (minus - odd_q)
    return tuple(out)


RIMS = [(1, 0, 0, 0, 2), (-1, 0, 2, 2, 2), (0, 1, 4, 4, 1), (0, -1, 5, 5, 1)]
RIMS += [(1, 1, 4, 6, 1), (1, -1, 5, 7, 1), (-1, 1, 4, 8, 1), (-1, -1, 5, 9, 1)]
CORNER = {(dx, dy): dst for dx, dy, src, dst, count in RIMS[4:]}
SIDES = [(dx, dy) for dy in (1, -1) for dx in (0, 1, -1)]
REACH = 3
HALOS = 2 * STEPS
PARTIALS = 2 * STEPS - 1


def near_offsets(size, reach):
    return sorted({d % size for d in range(-reach, reach + 1)})


def rim_copies(nx, ny):
    copies = []
    for dx, dy, src, dst, count in RIMS:
        where = (dx % nx, dy % ny)
        if copies:
            last, s, d, c = copies[-1]
            if last == where and s + c == src and d + c == dst:
                copies[-1] = (last, s, d, c + count)
                continue
        copies.append((where, src, dst, count))
    return copies


def thirds(value):
    high = value.astype(jnp.bfloat16).astype(jnp.float32)
    rest = value - high
    middle = rest.astype(jnp.bfloat16).astype(jnp.float32)
    parts = [high, middle, rest - middle, jnp.zeros_like(value)]
    return jnp.concatenate(parts, axis=0).astype(jnp.bfloat16)


def join_thirds(product):
    rows = product.shape[0] // 4
    return product[:rows] + (product[rows : 2 * rows] + product[2 * rows : 3 * rows])


def kernel(nx, ny, checkpoint, cotangent, area, cell, grad, area_grad, flats, spread, grads,
           ext_x, ext_y, halo_out, halo_in, rim_out, rim_in, part_out, part_in, sum_out, sum_a, sum_b,
           halo_sent, halo_got, rim_sent, rim_got, part_sent, part_got, sum_sent, sum_got):
    ix, iy = lax.axis_index("gx"), lax.axis_index("gy")
    near = [(dx, dy) for dx in near_offsets(nx, REACH) for dy in near_offsets(ny, REACH)]
    near = [o for o in near if o != (0, 0)]
    near.sort(key=lambda o: (-min(o[0], nx - o[0]), -min(o[1], ny - o[1])))
    low = SUBCELLS
    group = [(a, b) for a in range(low) for b in range(ny) if (a, b) != (0, 0)]
    far = list(range(1, nx // low))

    def at(dx, dy):
        return (lax.rem(ix + dx, nx), lax.rem(iy + dy, ny))

    base = lax.rem(ix, low)

    def in_group(a, b):
        return (ix - base + lax.rem(base + a, low), lax.rem(iy + b, ny))

    def in_far(c):
        return (lax.rem(ix + low * c, nx), iy)

    targets = [at(*o) for o in near] + [in_group(*o) for o in group] + [in_far(c) for c in far]
    barrier = pltpu.get_barrier_semaphore()
    for target in targets:
        pl.semaphore_signal(barrier, inc=1, device_id=target, device_id_type=MESH)

    rows, span = checkpoint.shape[1:]
    half = span - LANES
    row = lax.broadcasted_iota(jnp.int32, (rows, span), 0)
    lane = lax.broadcasted_iota(jnp.int32, (rows, span), 1)
    z = lax.bitwise_and(lane, NZ - 1)
    first_z, last_z = z == 0, z == NZ - 1
    row_h = lax.broadcasted_iota(jnp.int32, (rows, LANES), 0)
    lane_h = lax.broadcasted_iota(jnp.int32, (rows, LANES), 1)
    slot_h = lax.shift_right_logical(lane_h, 4)
    row_t = lax.broadcasted_iota(jnp.int32, (NTURB, LANES), 0)
    lane_t = lax.broadcasted_iota(jnp.int32, (NTURB, LANES), 1)

    def turned(value, shift, axis):
        shift = shift % value.shape[axis]
        return pltpu.roll(value, shift, axis) if shift else value

    def edge_of(sign):
        return rows - 1 if sign == 1 else 0

    def rim_lane(sign):
        return LANES - NZ if sign == 1 else 0

    def side_of(value, sign):
        return value[:, half:] if sign == 1 else value[:, :LANES]

    def pack_x(values, sign):
        packed = jnp.zeros((rows, span), jnp.float32)
        for k, value in enumerate(values):
            packed = jnp.where(row == k, turned(value, k - edge_of(sign), 0), packed)
        return packed

    def pack_y(values, sign):
        packed = jnp.zeros((rows, LANES), jnp.float32)
        for k, value in enumerate(values):
            moved = turned(side_of(value, sign), NZ * k - rim_lane(sign), 1)
            packed = jnp.where(slot_h == k, moved, packed)
        return packed

    def send_halo(f, fields, e):
        for sign, start in ((1, 0), (-1, 2)):
            packed = pack_x([f[i] for i in moving(0, sign)] + fields, sign)
            halo_out[e, start] = packed[:, :LANES]
            halo_out[e, start + 1] = packed[:, half:]
        for sign, start in ((1, 4), (-1, 5)):
            halo_out[e, start] = pack_y([f[i] for i in moving(1, sign)] + fields, sign)
        for where, src, dst, count in rim_copies(nx, ny):
            pltpu.make_async_remote_copy(
                src_ref=halo_out.at[e, pl.ds(src, count)],
                dst_ref=halo_in.at[e, pl.ds(dst, count)],
                send_sem=halo_sent.at[e], recv_sem=halo_got.at[e],
                device_id=at(*where), device_id_type=MESH).start()

    def receive(e, count):
        pltpu.make_async_copy(halo_in.at[e], halo_in.at[e], halo_got.at[e]).wait()
        from_x, from_y = {}, {}
        fields_x = [None] * count
        fields_y = [jnp.zeros((rows, LANES), jnp.float32)] * count
        for sign, start in ((1, 0), (-1, 2)):
            got = jnp.concatenate([halo_in[e, start], halo_in[e, start + 1]], axis=1)
            for k, i in enumerate(moving(0, sign)):
                from_x[i] = turned(got, edge_of(sign) - k, 0)
            for k in range(count):
                value = turned(got, edge_of(sign) - 5 - k, 0)
                fields_x[k] = value if sign == 1 else jnp.where(row == 0, value, fields_x[k])
        for side, (dx, dy) in enumerate(SIDES):
            got = halo_in[e, 4 if dy == 1 else 5]
            if dx:
                got = jnp.where(row_h == edge_of(dx), halo_in[e, CORNER[(dx, dy)]], got)
            for k, i in enumerate(moving(1, dy)):
                if VEC[i][0] == dx:
                    from_y[i] = turned(got, rim_lane(dy) - NZ * k, 1)
            for k in range(count):
                value = turned(got, NZ * (side - 5 - k), 1)
                fields_y[k] = jnp.where(slot_h == side, value, fields_y[k])
        return from_x, from_y, fields_x, fields_y

    def run(f, from_x, from_y):
        out = {}
        for i in f:
            dx, dy, dz = VEC[i]
            value = f[i]
            if dx:
                value = jnp.where(row == edge_of(dx), from_x[i], value)
            if dy == 1:
                edge = jnp.where(lane_h >= LANES - NZ, from_y[i], value[:, half:])
                value = jnp.concatenate([value[:, :half], edge], axis=1)
            elif dy == -1:
                edge = jnp.where(lane_h < NZ, from_y[i], value[:, :LANES])
                value = jnp.concatenate([edge, value[:, LANES:]], axis=1)
            value = turned(turned(value, dx, 0), NZ * dy + dz, 1)
            if dz:
                value = jnp.where(first_z if dz == 1 else last_z, f[OPP[i]], value)
            out[i] = value
        return out

    def pulls_of(rate):
        lines = [jnp.broadcast_to(rate[t : t + 1], (rows, LANES)) for t in range(NTURB)]
        wides = [jnp.concatenate([line] * (span // LANES), axis=1) for line in lines]
        return (total([spread[t] * wides[t] for t in range(NTURB)]),
                total([ext_x[t] * wides[t] for t in range(NTURB)]),
                total([ext_y[t] * lines[t] for t in range(NTURB)]))

    def run_added(entries, correct, fields, fields_x, fields_y, pulls):
        add = correct(fields, [p[0] for p in pulls])
        add_x = correct(fields_x, [p[1] for p in pulls])
        add_y = correct(fields_y, [p[2] for p in pulls])
        from_x = {i: add_x(i) for i in entries if VEC[i][0]}
        from_y = {}
        for side, (dx, dy) in enumerate(SIDES):
            inside = [i for i in entries if VEC[i][:2] == (dx, dy)]
            if inside:
                value = turned(add_y(inside[0]), rim_lane(dy) - NZ * side, 1)
                from_y.update({i: value for i in inside})
        return run({i: add(i) for i in entries}, from_x, from_y)

    def turbine_sums(value):
        sums = []
        for t in range(NTURB):
            prod = spread[t] * value
            sums.append(jnp.sum(prod[:, :LANES] + prod[:, half:], axis=0, keepdims=True))
        sums = jnp.sum(jnp.concatenate(sums, axis=0), axis=1, keepdims=True)
        return jnp.broadcast_to(sums, (NTURB, LANES))

    def send_partials(sums, e):
        width = LANES // (2 * len(sums))
        packed = sums[-1][8:]
        pieces = [s[h : h + 8] for s in sums for h in (0, 8)]
        for k in range(len(pieces) - 2, -1, -1):
            packed = jnp.where(lane_h < width * (k + 1), pieces[k], packed)
        part_out[e] = packed
        for k, (dx, dy) in enumerate(near):
            pltpu.make_async_remote_copy(
                src_ref=part_out.at[e], dst_ref=part_in.at[e, k],
                send_sem=part_sent.at[e], recv_sem=part_got.at[e],
                device_id=at(dx, dy), device_id_type=MESH).start()

    def take_partials(count, e):
        width = LANES // (2 * count)
        pltpu.make_async_copy(part_in.at[e], part_in.at[e], part_got.at[e]).wait()
        both = total([part_out[e]] + [part_in[e, k] for k in range(len(near))])
        pieces = []
        for k in range(2 * count):
            inside = (lane_h >= width * k) & (lane_h < width * (k + 1))
            piece, shift = jnp.where(inside, both, 0.0), width
            while shift < LANES:
                piece, shift = piece + pltpu.roll(piece, shift, 1), 2 * shift
            pieces.append(piece)
        return [jnp.concatenate(pieces[2 * k : 2 * k + 2], axis=0) / denom for k in range(count)]

    def wide(value, t):
        line = jnp.broadcast_to(value[t : t + 1], (rows, LANES))
        return jnp.concatenate([line] * (span // LANES), axis=1)

    def onehots(t):
        index = cell[t : t + 1, :]
        across = lax.shift_right_arithmetic(index, 8)
        along = lax.bitwise_and(index, 255)
        pick_x = lax.broadcasted_iota(jnp.int32, (rows, LANES), 0) == across
        pick_j = lax.broadcasted_iota(jnp.int32, (span, LANES), 0) == along
        return pick_x, jnp.where(pick_j, 1.0, 0.0).astype(jnp.bfloat16)

    def at_points(fields):
        lines = []
        for t in range(NTURB):
            pick_x, pick_j = onehots(t)
            found = join_thirds(jnp.dot(thirds(fields(t)), pick_j, preferred_element_type=jnp.float32))
            lines.append(jnp.sum(jnp.where(pick_x, found, 0.0), axis=0, keepdims=True))
        return jnp.concatenate(lines, axis=0)

    def sum_first(value, r):
        sum_out[r, 0] = value
        for k, (a, b) in enumerate(group):
            pltpu.make_async_remote_copy(
                src_ref=sum_out.at[r, 0], dst_ref=sum_a.at[r, k], send_sem=sum_sent.at[2 * r],
                recv_sem=sum_got.at[2 * r], device_id=in_group(a, b), device_id_type=MESH).start()

    def sum_second(r):
        pltpu.make_async_copy(sum_a.at[r], sum_a.at[r], sum_got.at[2 * r]).wait()
        sum_out[r, 1] = total([sum_out[r, 0]] + [sum_a[r, k] for k in range(len(group))])
        for k, c in enumerate(far):
            pltpu.make_async_remote_copy(
                src_ref=sum_out.at[r, 1], dst_ref=sum_b.at[r, k], send_sem=sum_sent.at[2 * r + 1],
                recv_sem=sum_got.at[2 * r + 1], device_id=in_far(c), device_id_type=MESH).start()

    def sum_last(r):
        pltpu.make_async_copy(sum_b.at[r], sum_b.at[r], sum_got.at[2 * r + 1]).wait()
        return total([sum_out[r, 1]] + [sum_b[r, k] for k in range(len(far))])

    field = [checkpoint[i] for i in range(19)]
    pl.semaphore_wait(barrier, len(targets))
    send_halo(field, [], 0)

    for t in range(NTURB):
        pick_x, pick_j = onehots(t)
        weight = jnp.where(pick_x, area[t : t + 1, :], 0.0)
        spread[t] = join_thirds(lax.dot_general(
            thirds(weight), pick_j, (((1,), (1,)), ((), ())), preferred_element_type=jnp.float32))
    denom = jnp.broadcast_to(jnp.sum(area[...], axis=1, keepdims=True), (NTURB, LANES))
    for h in range(2):
        mine = [spread[8 * h + k] for k in range(8)]
        for sign, start in ((1, 0), (-1, 4)):
            packed = pack_x(mine, sign)
            rim_out[start + 2 * h] = packed[:, :LANES]
            rim_out[start + 2 * h + 1] = packed[:, half:]
        for sign, start in ((1, 8), (-1, 10)):
            rim_out[start + h] = pack_y(mine, sign)
    for where, src, dst, count in rim_copies(nx, ny):
        pltpu.make_async_remote_copy(
            src_ref=rim_out.at[pl.ds(2 * src, 2 * count)],
            dst_ref=rim_in.at[pl.ds(2 * dst, 2 * count)],
            send_sem=rim_sent.at[0], recv_sem=rim_got.at[0],
            device_id=at(*where), device_id_type=MESH).start()

    def extend_spread():
        pltpu.make_async_copy(rim_in, rim_in, rim_got.at[0]).wait()
        sides = []
        for dx, dy in SIDES:
            pair = []
            for h in range(2):
                value = rim_in[(8 if dy == 1 else 10) + h]
                if dx:
                    corner = rim_in[2 * CORNER[(dx, dy)] + h]
                    value = jnp.where(row_h == edge_of(dx), corner, value)
                pair.append(value)
            sides.append(pair)
        for h in range(2):
            ups = jnp.concatenate([rim_in[2 * h], rim_in[2 * h + 1]], axis=1)
            downs = jnp.concatenate([rim_in[4 + 2 * h], rim_in[5 + 2 * h]], axis=1)
            for k in range(8):
                up, down = turned(ups, rows - 1 - k, 0), turned(downs, -k, 0)
                ext_x[8 * h + k] = jnp.where(row == rows - 1, up, jnp.where(row == 0, down, 0.0))
                packed = jnp.zeros((rows, LANES), jnp.float32)
                for side, pair in enumerate(sides):
                    moved = turned(pair[h], NZ * (side - k), 1)
                    packed = jnp.where(slot_h == side, moved, packed)
                ext_y[8 * h + k] = packed

    def forced(fields, pulls):
        force = -THRUST * fields[0] * pulls[0]
        return lambda i: PUSH[i] * force

    def speed_fixed(fields, pulls):
        speed_bar = fields[1] * pulls[0] + fields[2] * pulls[1]
        parts = {c: (float(-c) - fields[0]) * speed_bar for c in (-1, 0, 1)}
        return lambda i: parts[VEC[i][0]]

    rotors, speeds, pulls = [], [], []
    from_x, from_y, unused_x, unused_y = receive(0, 0)
    flat = run(dict(enumerate(field)), from_x, from_y)
    pushed_on = [i for i in range(19) if PUSH[i] != 0.0]
    for s in range(STEPS):
        flat = [flat[i] for i in range(19)]
        for i in range(19):
            flats[s, i] = flat[i]
        speed = momentum_of(flat, 0) / density_of(flat)
        speeds.append(speed)
        if s == STEPS - 1:
            break
        send_partials([turbine_sums(speed)], s)
        moved = collide(*flat)
        send_halo(moved, [speed], s + 1)
        if s == 0:
            extend_spread()
        from_x, from_y, fields_x, fields_y = receive(s + 1, 1)
        flat = run(dict(enumerate(moved)), from_x, from_y)
        rotors.append(take_partials(1, s)[0])
        pulls.append(pulls_of(rotors[s]))
        added = run_added(pushed_on, forced, [speed], fields_x, fields_y, [pulls[s]])
        flat.update({i: flat[i] + added[i] for i in pushed_on})

    adjoint = [cotangent[i] for i in range(19)]
    for n in range(STEPS):
        s, e = STEPS - 1 - n, STEPS + n
        flat = [flats[s, i] for i in range(19)]
        speed = speeds[s]
        force_bar = weighted(PUSH, adjoint)
        load = -THRUST * force_bar * speed
        load_sums = turbine_sums(load)
        if n == 0:
            send_partials([turbine_sums(speed), load_sums], s)
        else:
            send_partials([load_sums], s + 2 * n)
        if n == STEPS - 1:
            rotor = rotors[s]
            found = at_points(lambda t: grads[t] + wide(rotor, t) * load)
            sum_first(jnp.where(lane_t < PTS, found, load_sums), 1)
        unused, pullback = jax.vjp(collide, *flat)
        flat_bar = pullback(tuple(adjoint))
        inverse = 1.0 / density_of(flat)
        fields = [speed, inverse, -THRUST * force_bar * inverse]
        turned_bar = [flat_bar[OPP[i]] for i in range(19)]
        send_halo(turned_bar, fields, e)
        if n == 0:
            sum_first(at_points(lambda t: speeds[0] - wide(rotors[0], t)), 0)
        elif n == 1:
            sum_second(0)
        if n == STEPS - 1:
            sum_second(1)
        from_x, from_y, fields_x, fields_y = receive(e, 3)
        pushed = run(dict(enumerate(turned_bar)), from_x, from_y)
        if n == 0:
            rotor, numer_bar = take_partials(2, s)
            pulls.append(pulls_of(rotor))
        else:
            rotor = rotors[s]
            numer_bar = take_partials(1, s + 2 * n)[0]
        added = run_added(range(19), speed_fixed, fields, fields_x, fields_y, [pulls_of(numer_bar), pulls[s]])
        adjoint = [pushed[OPP[i]] + added[OPP[i]] for i in range(19)]
        if n < STEPS - 1:
            for t in range(NTURB):
                turn = wide(rotor, t)
                part = turn * load + wide(numer_bar, t) * (speed - turn)
                grads[t] = part if n == 0 else grads[t] + part

    for i in range(19):
        grad[i] = adjoint[i]
    spread_of = sum_last(0)
    sums = sum_last(1)
    numer_bar = jnp.broadcast_to(sums[:, PTS : PTS + 1], (NTURB, LANES)) / denom
    area_grad[...] = sums + numer_bar * spread_of

    for e in range(HALOS):
        pltpu.make_async_copy(halo_in.at[e], halo_in.at[e], halo_sent.at[e]).wait()
    for e in range(PARTIALS):
        pltpu.make_async_copy(part_in.at[e], part_in.at[e], part_sent.at[e]).wait()
    pltpu.make_async_copy(rim_in, rim_in, rim_sent.at[0]).wait()
    for r in range(2):
        pltpu.make_async_copy(sum_a.at[r], sum_a.at[r], sum_sent.at[2 * r]).wait()
        pltpu.make_async_copy(sum_b.at[r], sum_b.at[r], sum_sent.at[2 * r + 1]).wait()


def body(checkpoint, cotangent, blade_area, hub_tile, point_side, point_local):
    nx, ny = lax.axis_size("gx"), lax.axis_size("gy")
    ix, iy = lax.axis_index("gx"), lax.axis_index("gy")
    pops, rows, span = checkpoint.shape
    side = point_side.reshape(NTURB, PTS)
    tile_x = (hub_tile[:, None] // ny + side // 3 - 1) % nx
    tile_y = (hub_tile[:, None] % ny + side % 3 - 1) % ny
    mine = (tile_x == ix) & (tile_y == iy)
    cell = jnp.where(mine, point_local.reshape(NTURB, PTS), -1)
    pad = ((0, 0), (0, LANES - PTS))
    cell = jnp.pad(cell, pad, constant_values=-1)
    area = jnp.pad(blade_area.reshape(NTURB, PTS), pad)
    near = len(near_offsets(nx, REACH)) * len(near_offsets(ny, REACH)) - 1
    group, far = SUBCELLS * ny - 1, nx // SUBCELLS - 1
    f32, dma = jnp.float32, pltpu.SemaphoreType.DMA
    tile, vreg = (rows, span), (rows, LANES)
    shapes = [(STEPS, pops) + tile] + [(NTURB,) + tile] * 3 + [(NTURB,) + vreg]
    shapes += [(HALOS, 6) + vreg, (HALOS, 10) + vreg, (12,) + vreg, (20,) + vreg]
    shapes += [(PARTIALS,) + vreg, (PARTIALS, near) + vreg]
    shapes += [(2, 2, NTURB, LANES), (2, group, NTURB, LANES), (2, far, NTURB, LANES)]
    whole = pl.BlockSpec(memory_space=pltpu.VMEM)
    adjoint, grads = pl.pallas_call(
        functools.partial(kernel, nx, ny),
        out_shape=(jax.ShapeDtypeStruct(checkpoint.shape, f32),
                   jax.ShapeDtypeStruct((NTURB, LANES), f32)),
        in_specs=[whole] * 4,
        out_specs=(whole, whole),
        scratch_shapes=[pltpu.VMEM(shape, f32) for shape in shapes]
        + [dma((HALOS,))] * 2 + [dma((1,))] * 2 + [dma((PARTIALS,))] * 2 + [dma((4,))] * 2,
        compiler_params=pltpu.CompilerParams(
            collective_id=0, has_side_effects=True, vmem_limit_bytes=32 * 1024 * 1024),
    )(checkpoint, cotangent, area, cell)
    return adjoint, grads[:, :PTS].reshape(NTURB * PTS)


def solution(mesh):
    return jax.shard_map(
        body,
        mesh=mesh,
        in_specs=(P(None, "gx", "gy"), P(None, "gx", "gy"), P(), P(), P(), P()),
        out_specs=(P(None, "gx", "gy"), P()),
        check_vma=False,
    )
```

```python
import functools

import jax
import jax.numpy as jnp
import numpy as np
from jax import lax
from jax.experimental import pallas as pl
from jax.experimental.pallas import tpu as pltpu
from jax.sharding import PartitionSpec as P

NZ = 16
STEPS = 4
NTURB = 16
PTS = 96
LANES = 128
SUBCELLS = 4

TAU_ZERO = 0.52
SMAGORINSKY = 0.17 * 0.17
TINY = 1e-10
THRUST = 4.0
GHOST_RATES = np.array([1.05, 1.15, 1.25, 1.35, 1.45, 1.55, 1.65, 1.75, 1.85])
MESH = pl.DeviceIdType.MESH


def lattice():
    axis_part = [(1, 0, 0), (-1, 0, 0), (0, 1, 0), (0, -1, 0), (0, 0, 1), (0, 0, -1)]
    edge_part = [
        (1, 1, 0),
        (-1, -1, 0),
        (1, -1, 0),
        (-1, 1, 0),
        (1, 0, 1),
        (-1, 0, -1),
        (1, 0, -1),
        (-1, 0, 1),
        (0, 1, 1),
        (0, -1, -1),
        (0, 1, -1),
        (0, -1, 1),
    ]
    vectors = np.array([(0, 0, 0)] + axis_part + edge_part) * 1.0
    weights = np.array([1.0 / 3.0] + [1.0 / 18.0] * 6 + [1.0 / 36.0] * 12)
    opposite = np.array(
        [int(np.argmin(np.abs(vectors + vectors[column]).sum(1))) for column in range(19)]
    )
    return (vectors, weights, opposite)


def orthonormal(monomials, weights):
    rows = []
    for entry in monomials:
        vector = entry * 1.0
        for sweep in range(2):
            for other in rows:
                vector = vector - np.sum(weights * vector * other) * other
        vector = vector / np.sqrt(np.sum(weights * vector * vector))
        rows.append(vector)
    return np.stack(rows, 0)


def basis_table():
    vectors, weights, opposite = lattice()
    x, y, z = (vectors[:, 0], vectors[:, 1], vectors[:, 2])
    monomials = [np.ones(19), x, y, z, x * x, y * y, z * z, x * y, x * z, y * z]
    monomials += [x * y * y, x * z * z, y * x * x, y * z * z, z * x * x, z * y * y]
    monomials += [x * x * y * y, x * x * z * z, y * y * z * z]
    return orthonormal(monomials, weights)


VECTORS, WEIGHTS, OPPOSITE = lattice()
BASIS = basis_table()
VEC = [tuple(int(c) for c in row) for row in VECTORS]
INDEX = {vec: i for i, vec in enumerate(VEC)}
OPP = [int(i) for i in OPPOSITE]
PUSH = [float(p) for p in 3.0 * WEIGHTS * VECTORS[:, 0]]


def moving(axis, sign):
    return [i for i in range(19) if VEC[i][axis] == sign]


def total(values):
    values = list(values)
    while len(values) > 1:
        pairs = [values[k] + values[k + 1] for k in range(0, len(values) - 1, 2)]
        values = pairs + values[len(values) - len(values) % 2 :]
    return values[0]


def weighted(coefs, values):
    return total([float(c) * v for c, v in zip(coefs, values) if abs(c) > 1e-9])


def density_of(f):
    return total(f)


def momentum_of(f, axis):
    return total(f[i] for i in moving(axis, 1)) - total(f[i] for i in moving(axis, -1))


def collide(*f):
    rho = density_of(f)
    mom = [momentum_of(f, a) for a in range(3)]
    inv = 1.0 / rho
    even = {0: f[0]}
    planes = [(0, 1), (0, 2), (1, 2)]
    unit = np.eye(3, dtype=int)
    diff, cross = {}, {}
    for a in range(3):
        p = INDEX[tuple(unit[a])]
        even[a + 1] = f[p] + f[OPP[p]]
        diff[(a,)] = f[p] - f[OPP[p]]
    for k, (a, b) in enumerate(planes):
        p, q = INDEX[tuple(unit[a] + unit[b])], INDEX[tuple(unit[a] - unit[b])]
        sp, sq = f[p] + f[OPP[p]], f[q] + f[OPP[q]]
        dp, dq = f[p] - f[OPP[p]], f[q] - f[OPP[q]]
        even[4 + k] = sp + sq
        cross[k] = sp - sq
        diff[(a, b)] = dp + dq
        diff[(b, a)] = dp - dq
    stress = []
    for a in range(3):
        near = [4 + k for k, pl_ in enumerate(planes) if a in pl_]
        second = even[a + 1] + even[near[0]] + even[near[1]]
        stress.append(second - rho * (1.0 / 3.0) - mom[a] * mom[a] * inv)
    for k, (a, b) in enumerate(planes):
        stress.append(cross[k] - mom[a] * mom[b] * inv)
    square = total([p * p for p in stress[:3]]) + 2.0 * total([p * p for p in stress[3:]])
    tau = 0.5 * (
        TAU_ZERO
        + jnp.sqrt(TAU_ZERO * TAU_ZERO + 18.0 * SMAGORINSKY * jnp.sqrt(square + TINY) * inv)
    )
    rate = 1.0 / tau
    relaxed = [p * rate for p in stress]
    trace = (relaxed[0] + relaxed[1] + relaxed[2]) * (1.0 / 3.0)
    members = [0] + [INDEX[tuple(unit[a])] for a in range(3)]
    members += [INDEX[tuple(unit[a] + unit[b])] for a, b in planes]
    ghosts = [weighted(BASIS[r][members], [even[c] for c in range(7)]) for r in (16, 17, 18)]
    drop_even = []
    for c, m in enumerate(members):
        part = weighted([WEIGHTS[m] * GHOST_RATES[r - 10] * BASIS[r][m] for r in (16, 17, 18)], ghosts)
        if c == 0:
            aniso = -trace
        elif c < 4:
            aniso = relaxed[c - 1] - trace
        else:
            a, b = planes[c - 4]
            aniso = relaxed[a] + relaxed[b] - trace
        drop_even.append(part + float(4.5 * WEIGHTS[m]) * aniso)
    drop_odd = {}
    for a in range(3):
        others = [b for b in range(3) if b != a]
        kinds = [(a,)] + [(a, b) for b in others]
        reps = [INDEX[tuple(unit[a])]] + [INDEX[tuple(unit[a] + unit[b])] for b in others]
        rows = (10 + 2 * a, 11 + 2 * a)
        odd = [weighted(BASIS[r][reps], [diff[k] for k in kinds]) for r in rows]
        for kind, m in zip(kinds, reps):
            drop_odd[kind] = weighted([WEIGHTS[m] * GHOST_RATES[r - 10] * BASIS[r][m] for r in rows], odd)
    out = [None] * 19
    out[0] = f[0] - drop_even[0]
    for a in range(3):
        p = INDEX[tuple(unit[a])]
        out[p] = f[p] - (drop_even[a + 1] + drop_odd[(a,)])
        out[OPP[p]] = f[OPP[p]] - (drop_even[a + 1] - drop_odd[(a,)])
    for k, (a, b) in enumerate(planes):
        p, q = INDEX[tuple(unit[a] + unit[b])], INDEX[tuple(unit[a] - unit[b])]
        shear = 0.25 * relaxed[3 + k]
        plus, minus = drop_even[4 + k] + shear, drop_even[4 + k] - shear
        odd_p = drop_odd[(a, b)] + drop_odd[(b, a)]
        odd_q = drop_odd[(a, b)] - drop_odd[(b, a)]
        out[p] = f[p] - (plus + odd_p)
        out[OPP[p]] = f[OPP[p]] - (plus - odd_p)
        out[q] = f[q] - (minus + odd_q)
        out[OPP[q]] = f[OPP[q]] - (minus - odd_q)
    return tuple(out)


RIMS = [(1, 0, 0, 2), (-1, 0, 2, 2), (0, 1, 4, 1), (0, -1, 5, 1)]
CORNERS = [(1, 1, 0, 1), (1, -1, 1, 1), (-1, 1, 2, 1), (-1, -1, 3, 1)]
CORNER = {(dx, dy): slot for dx, dy, slot, count in CORNERS}
SIDES = [(dx, dy) for dy in (1, -1) for dx in (0, 1, -1)]
REACH = 3
HALOS = 2 * STEPS
PARTIALS = 2 * STEPS - 1


def near_offsets(size, reach):
    return sorted({d % size for d in range(-reach, reach + 1)})


def merged(rims, nx, ny):
    copies = []
    for dx, dy, slot, count in rims:
        where = (dx % nx, dy % ny)
        if copies and copies[-1][0] == where:
            copies[-1] = (where, copies[-1][1], copies[-1][2] + count)
        else:
            copies.append((where, slot, count))
    return copies


def thirds(value):
    high = value.astype(jnp.bfloat16).astype(jnp.float32)
    rest = value - high
    middle = rest.astype(jnp.bfloat16).astype(jnp.float32)
    parts = [high, middle, rest - middle, jnp.zeros_like(value)]
    return jnp.concatenate(parts, axis=0).astype(jnp.bfloat16)


def join_thirds(product):
    rows = product.shape[0] // 4
    return product[:rows] + (product[rows : 2 * rows] + product[2 * rows : 3 * rows])


def kernel(nx, ny, checkpoint, cotangent, area, cell, grad, area_grad, flats, spread, grads,
           ext_x, ext_y, halo_out, halo_in, rim_out, rim_in, turn_out, turn_in, rim_turn_out, rim_turn_in, part_out, part_in, sum_out, sum_a, sum_b,
           halo_sent, halo_got, rim_sent, rim_got, turn_sent, turn_got, part_sent, part_got, sum_sent, sum_got):
    ix, iy = lax.axis_index("gx"), lax.axis_index("gy")
    near = [(dx, dy) for dx in near_offsets(nx, REACH) for dy in near_offsets(ny, REACH)]
    near = [o for o in near if o != (0, 0)]
    near.sort(key=lambda o: (-min(o[0], nx - o[0]), -min(o[1], ny - o[1])))
    low = SUBCELLS
    group = [(a, b) for a in range(low) for b in range(ny) if (a, b) != (0, 0)]
    far = list(range(1, nx // low))

    def at(dx, dy):
        return (lax.rem(ix + dx, nx), lax.rem(iy + dy, ny))

    base = lax.rem(ix, low)

    def in_group(a, b):
        return (ix - base + lax.rem(base + a, low), lax.rem(iy + b, ny))

    def in_far(c):
        return (lax.rem(ix + low * c, nx), iy)

    targets = [at(*o) for o in near] + [in_group(*o) for o in group] + [in_far(c) for c in far]
    barrier = pltpu.get_barrier_semaphore()
    for target in targets:
        pl.semaphore_signal(barrier, inc=1, device_id=target, device_id_type=MESH)

    rows, span = checkpoint.shape[1:]
    half = span - LANES
    row = lax.broadcasted_iota(jnp.int32, (rows, span), 0)
    lane = lax.broadcasted_iota(jnp.int32, (rows, span), 1)
    z = lax.bitwise_and(lane, NZ - 1)
    first_z, last_z = z == 0, z == NZ - 1
    row_h = lax.broadcasted_iota(jnp.int32, (rows, LANES), 0)
    lane_h = lax.broadcasted_iota(jnp.int32, (rows, LANES), 1)
    slot_h = lax.shift_right_logical(lane_h, 4)
    row_t = lax.broadcasted_iota(jnp.int32, (NTURB, LANES), 0)
    lane_t = lax.broadcasted_iota(jnp.int32, (NTURB, LANES), 1)

    def turned(value, shift, axis):
        shift = shift % value.shape[axis]
        return pltpu.roll(value, shift, axis) if shift else value

    def edge_of(sign):
        return rows - 1 if sign == 1 else 0

    def rim_lane(sign):
        return LANES - NZ if sign == 1 else 0

    def side_of(value, sign):
        return value[:, half:] if sign == 1 else value[:, :LANES]

    def pack_x(values, sign):
        packed = jnp.zeros((rows, span), jnp.float32)
        for k, value in enumerate(values):
            packed = jnp.where(row == k, turned(value, k - edge_of(sign), 0), packed)
        return packed

    def pack_y(values, sign):
        packed = jnp.zeros((rows, LANES), jnp.float32)
        for k, value in enumerate(values):
            moved = turned(side_of(value, sign), NZ * k - rim_lane(sign), 1)
            packed = jnp.where(slot_h == k, moved, packed)
        return packed

    def send_halo(f, fields, e):
        for sign, start in ((1, 0), (-1, 2)):
            packed = pack_x([f[i] for i in moving(0, sign)] + fields, sign)
            halo_out[e, start] = packed[:, :LANES]
            halo_out[e, start + 1] = packed[:, half:]
        for sign, start in ((1, 4), (-1, 5)):
            halo_out[e, start] = pack_y([f[i] for i in moving(1, sign)] + fields, sign)
            for dx in (1, -1):
                edge = edge_of(dx)
                turn_out[e, CORNER[(dx, sign)]] = halo_out[e, start, edge : edge + 1]
        send_rims(halo_out.at[e], halo_in.at[e], turn_out.at[e], turn_in.at[e], 1,
                  (halo_sent.at[e], halo_got.at[e], turn_sent.at[e], turn_got.at[e]))

    def send_rims(out, into, turn, into_turn, scale, sems):
        for rims, source, target, sent, got in ((RIMS, out, into) + sems[:2], (CORNERS, turn, into_turn) + sems[2:]):
            for where, slot, count in merged(rims, nx, ny):
                part = pl.ds(scale * slot, scale * count)
                pltpu.make_async_remote_copy(
                    src_ref=source.at[part], dst_ref=target.at[part], send_sem=sent, recv_sem=got,
                    device_id=at(*where), device_id_type=MESH).start()

    def receive(e, count):
        pltpu.make_async_copy(halo_in.at[e], halo_in.at[e], halo_got.at[e]).wait()
        pltpu.make_async_copy(turn_in.at[e], turn_in.at[e], turn_got.at[e]).wait()
        from_x, from_y = {}, {}
        fields_x = [None] * count
        fields_y = [jnp.zeros((rows, LANES), jnp.float32)] * count
        for sign, start in ((1, 0), (-1, 2)):
            got = jnp.concatenate([halo_in[e, start], halo_in[e, start + 1]], axis=1)
            for k, i in enumerate(moving(0, sign)):
                from_x[i] = turned(got, edge_of(sign) - k, 0)
            for k in range(count):
                value = turned(got, edge_of(sign) - 5 - k, 0)
                fields_x[k] = value if sign == 1 else jnp.where(row == 0, value, fields_x[k])
        for side, (dx, dy) in enumerate(SIDES):
            got = halo_in[e, 4 if dy == 1 else 5]
            if dx:
                got = jnp.where(row_h == edge_of(dx), turn_in[e, CORNER[(dx, dy)]], got)
            for k, i in enumerate(moving(1, dy)):
                if VEC[i][0] == dx:
                    from_y[i] = turned(got, rim_lane(dy) - NZ * k, 1)
            for k in range(count):
                value = turned(got, NZ * (side - 5 - k), 1)
                fields_y[k] = jnp.where(slot_h == side, value, fields_y[k])
        return from_x, from_y, fields_x, fields_y

    def run(f, from_x, from_y):
        out = {}
        for i in f:
            dx, dy, dz = VEC[i]
            value = f[i]
            if dx:
                value = jnp.where(row == edge_of(dx), from_x[i], value)
            if dy == 1:
                edge = jnp.where(lane_h >= LANES - NZ, from_y[i], value[:, half:])
                value = jnp.concatenate([value[:, :half], edge], axis=1)
            elif dy == -1:
                edge = jnp.where(lane_h < NZ, from_y[i], value[:, :LANES])
                value = jnp.concatenate([edge, value[:, LANES:]], axis=1)
            value = turned(turned(value, dx, 0), NZ * dy + dz, 1)
            if dz:
                value = jnp.where(first_z if dz == 1 else last_z, f[OPP[i]], value)
            out[i] = value
        return out

    def pulls_of(rate):
        lines = [jnp.broadcast_to(rate[t : t + 1], (rows, LANES)) for t in range(NTURB)]
        wides = [jnp.concatenate([line] * (span // LANES), axis=1) for line in lines]
        return (total([spread[t] * wides[t] for t in range(NTURB)]),
                total([ext_x[t] * wides[t] for t in range(NTURB)]),
                total([ext_y[t] * lines[t] for t in range(NTURB)]))

    def run_added(entries, correct, fields, fields_x, fields_y, pulls):
        add = correct(fields, [p[0] for p in pulls])
        add_x = correct(fields_x, [p[1] for p in pulls])
        add_y = correct(fields_y, [p[2] for p in pulls])
        from_x = {i: add_x(i) for i in entries if VEC[i][0]}
        from_y = {}
        for side, (dx, dy) in enumerate(SIDES):
            inside = [i for i in entries if VEC[i][:2] == (dx, dy)]
            if inside:
                value = turned(add_y(inside[0]), rim_lane(dy) - NZ * side, 1)
                from_y.update({i: value for i in inside})
        return run({i: add(i) for i in entries}, from_x, from_y)

    def turbine_sums(value):
        sums = []
        for t in range(NTURB):
            prod = spread[t] * value
            sums.append(jnp.sum(prod[:, :LANES] + prod[:, half:], axis=0, keepdims=True))
        sums = jnp.sum(jnp.concatenate(sums, axis=0), axis=1, keepdims=True)
        return jnp.broadcast_to(sums, (NTURB, LANES))

    def send_partials(sums, e):
        width = LANES // (NTURB * len(sums))
        packed = jnp.zeros((NTURB, LANES), jnp.float32)
        for c, value in enumerate(sums):
            packed = jnp.where(lane_t // width == row_t + NTURB * c, value, packed)
        part_out[e] = jnp.sum(packed, axis=0, keepdims=True)
        for k, (dx, dy) in enumerate(near):
            pltpu.make_async_remote_copy(
                src_ref=part_out.at[e], dst_ref=part_in.at[e, k],
                send_sem=part_sent.at[e], recv_sem=part_got.at[e],
                device_id=at(dx, dy), device_id_type=MESH).start()

    def take_partials(count, e):
        width = LANES // (NTURB * count)
        pltpu.make_async_copy(part_in.at[e], part_in.at[e], part_got.at[e]).wait()
        both = total([part_out[e]] + [part_in[e, k] for k in range(len(near))])
        both = jnp.broadcast_to(both, (NTURB, LANES))
        out = []
        for c in range(count):
            picked = jnp.where(lane_t == width * (row_t + NTURB * c), both, 0.0)
            line = jnp.sum(picked, axis=1, keepdims=True)
            out.append(jnp.broadcast_to(line, (NTURB, LANES)) / denom)
        return out

    def wide(value, t):
        line = jnp.broadcast_to(value[t : t + 1], (rows, LANES))
        return jnp.concatenate([line] * (span // LANES), axis=1)

    def onehots(t):
        index = cell[t : t + 1, :]
        across = lax.shift_right_arithmetic(index, 8)
        along = lax.bitwise_and(index, 255)
        pick_x = lax.broadcasted_iota(jnp.int32, (rows, LANES), 0) == across
        pick_j = lax.broadcasted_iota(jnp.int32, (span, LANES), 0) == along
        return pick_x, jnp.where(pick_j, 1.0, 0.0).astype(jnp.bfloat16)

    def at_points(fields):
        lines = []
        for t in range(NTURB):
            pick_x, pick_j = onehots(t)
            found = join_thirds(jnp.dot(thirds(fields(t)), pick_j, preferred_element_type=jnp.float32))
            lines.append(jnp.sum(jnp.where(pick_x, found, 0.0), axis=0, keepdims=True))
        return jnp.concatenate(lines, axis=0)

    def sum_first(value, r):
        sum_out[r, 0] = value
        for k, (a, b) in enumerate(group):
            pltpu.make_async_remote_copy(
                src_ref=sum_out.at[r, 0], dst_ref=sum_a.at[r, k], send_sem=sum_sent.at[2 * r],
                recv_sem=sum_got.at[2 * r], device_id=in_group(a, b), device_id_type=MESH).start()

    def sum_second(r):
        pltpu.make_async_copy(sum_a.at[r], sum_a.at[r], sum_got.at[2 * r]).wait()
        sum_out[r, 1] = total([sum_out[r, 0]] + [sum_a[r, k] for k in range(len(group))])
        for k, c in enumerate(far):
            pltpu.make_async_remote_copy(
                src_ref=sum_out.at[r, 1], dst_ref=sum_b.at[r, k], send_sem=sum_sent.at[2 * r + 1],
                recv_sem=sum_got.at[2 * r + 1], device_id=in_far(c), device_id_type=MESH).start()

    def sum_last(r):
        pltpu.make_async_copy(sum_b.at[r], sum_b.at[r], sum_got.at[2 * r + 1]).wait()
        return total([sum_out[r, 1]] + [sum_b[r, k] for k in range(len(far))])

    field = [checkpoint[i] for i in range(19)]
    pl.semaphore_wait(barrier, len(targets))
    send_halo(field, [], 0)

    for t in range(NTURB):
        pick_x, pick_j = onehots(t)
        weight = jnp.where(pick_x, area[t : t + 1, :], 0.0)
        spread[t] = join_thirds(lax.dot_general(
            thirds(weight), pick_j, (((1,), (1,)), ((), ())), preferred_element_type=jnp.float32))
    denom = jnp.broadcast_to(jnp.sum(area[...], axis=1, keepdims=True), (NTURB, LANES))
    for h in range(2):
        mine = [spread[8 * h + k] for k in range(8)]
        for sign, start in ((1, 0), (-1, 4)):
            packed = pack_x(mine, sign)
            rim_out[start + 2 * h] = packed[:, :LANES]
            rim_out[start + 2 * h + 1] = packed[:, half:]
        for sign, start in ((1, 8), (-1, 10)):
            rim_out[start + h] = pack_y(mine, sign)
    for sign, start in ((1, 8), (-1, 10)):
        for dx in (1, -1):
            for h in range(2):
                edge = edge_of(dx)
                rim_turn_out[2 * CORNER[(dx, sign)] + h] = rim_out[start + h, edge : edge + 1]
    send_rims(rim_out, rim_in, rim_turn_out, rim_turn_in, 2,
              (rim_sent.at[0], rim_got.at[0], rim_sent.at[1], rim_got.at[1]))

    def extend_spread():
        pltpu.make_async_copy(rim_in, rim_in, rim_got.at[0]).wait()
        pltpu.make_async_copy(rim_turn_in, rim_turn_in, rim_got.at[1]).wait()
        sides = []
        for dx, dy in SIDES:
            pair = []
            for h in range(2):
                value = rim_in[(8 if dy == 1 else 10) + h]
                if dx:
                    corner = rim_turn_in[2 * CORNER[(dx, dy)] + h]
                    value = jnp.where(row_h == edge_of(dx), corner, value)
                pair.append(value)
            sides.append(pair)
        for h in range(2):
            ups = jnp.concatenate([rim_in[2 * h], rim_in[2 * h + 1]], axis=1)
            downs = jnp.concatenate([rim_in[4 + 2 * h], rim_in[5 + 2 * h]], axis=1)
            for k in range(8):
                up, down = turned(ups, rows - 1 - k, 0), turned(downs, -k, 0)
                ext_x[8 * h + k] = jnp.where(row == rows - 1, up, jnp.where(row == 0, down, 0.0))
                packed = jnp.zeros((rows, LANES), jnp.float32)
                for side, pair in enumerate(sides):
                    moved = turned(pair[h], NZ * (side - k), 1)
                    packed = jnp.where(slot_h == side, moved, packed)
                ext_y[8 * h + k] = packed

    def forced(fields, pulls):
        force = -THRUST * fields[0] * pulls[0]
        return lambda i: PUSH[i] * force

    def speed_fixed(fields, pulls):
        speed_bar = fields[1] * pulls[0] + fields[2] * pulls[1]
        parts = {c: (float(-c) - fields[0]) * speed_bar for c in (-1, 0, 1)}
        return lambda i: parts[VEC[i][0]]

    rotors, speeds, pulls = [], [], []
    from_x, from_y, unused_x, unused_y = receive(0, 0)
    flat = run(dict(enumerate(field)), from_x, from_y)
    pushed_on = [i for i in range(19) if PUSH[i] != 0.0]
    for s in range(STEPS):
        flat = [flat[i] for i in range(19)]
        for i in range(19):
            flats[s, i] = flat[i]
        speed = momentum_of(flat, 0) / density_of(flat)
        speeds.append(speed)
        if s == STEPS - 1:
            break
        send_partials([turbine_sums(speed)], s)
        moved = collide(*flat)
        send_halo(moved, [speed], s + 1)
        if s == 0:
            extend_spread()
        from_x, from_y, fields_x, fields_y = receive(s + 1, 1)
        flat = run(dict(enumerate(moved)), from_x, from_y)
        rotors.append(take_partials(1, s)[0])
        pulls.append(pulls_of(rotors[s]))
        added = run_added(pushed_on, forced, [speed], fields_x, fields_y, [pulls[s]])
        flat.update({i: flat[i] + added[i] for i in pushed_on})

    adjoint = [cotangent[i] for i in range(19)]
    for n in range(STEPS):
        s, e = STEPS - 1 - n, STEPS + n
        flat = [flats[s, i] for i in range(19)]
        speed = speeds[s]
        force_bar = weighted(PUSH, adjoint)
        load = -THRUST * force_bar * speed
        load_sums = turbine_sums(load)
        if n == 0:
            send_partials([turbine_sums(speed), load_sums], s)
        else:
            send_partials([load_sums], s + 2 * n)
        if n == STEPS - 1:
            rotor = rotors[s]
            found = at_points(lambda t: grads[t] + wide(rotor, t) * load)
            sum_first(jnp.where(lane_t < PTS, found, load_sums), 1)
        unused, pullback = jax.vjp(collide, *flat)
        flat_bar = pullback(tuple(adjoint))
        inverse = 1.0 / density_of(flat)
        fields = [speed, inverse, -THRUST * force_bar * inverse]
        turned_bar = [flat_bar[OPP[i]] for i in range(19)]
        send_halo(turned_bar, fields, e)
        if n == 0:
            sum_first(at_points(lambda t: speeds[0] - wide(rotors[0], t)), 0)
        elif n == 1:
            sum_second(0)
        if n == STEPS - 1:
            sum_second(1)
        from_x, from_y, fields_x, fields_y = receive(e, 3)
        pushed = run(dict(enumerate(turned_bar)), from_x, from_y)
        if n == 0:
            rotor, numer_bar = take_partials(2, s)
            pulls.append(pulls_of(rotor))
        else:
            rotor = rotors[s]
            numer_bar = take_partials(1, s + 2 * n)[0]
        added = run_added(range(19), speed_fixed, fields, fields_x, fields_y, [pulls_of(numer_bar), pulls[s]])
        adjoint = [pushed[OPP[i]] + added[OPP[i]] for i in range(19)]
        if n < STEPS - 1:
            for t in range(NTURB):
                turn = wide(rotor, t)
                part = turn * load + wide(numer_bar, t) * (speed - turn)
                grads[t] = part if n == 0 else grads[t] + part

    for i in range(19):
        grad[i] = adjoint[i]
    spread_of = sum_last(0)
    sums = sum_last(1)
    numer_bar = jnp.broadcast_to(sums[:, PTS : PTS + 1], (NTURB, LANES)) / denom
    area_grad[...] = sums + numer_bar * spread_of

    for e in range(HALOS):
        pltpu.make_async_copy(halo_in.at[e], halo_in.at[e], halo_sent.at[e]).wait()
        pltpu.make_async_copy(turn_in.at[e], turn_in.at[e], turn_sent.at[e]).wait()
    for e in range(PARTIALS):
        pltpu.make_async_copy(part_in.at[e], part_in.at[e], part_sent.at[e]).wait()
    pltpu.make_async_copy(rim_in, rim_in, rim_sent.at[0]).wait()
    pltpu.make_async_copy(rim_turn_in, rim_turn_in, rim_sent.at[1]).wait()
    for r in range(2):
        pltpu.make_async_copy(sum_a.at[r], sum_a.at[r], sum_sent.at[2 * r]).wait()
        pltpu.make_async_copy(sum_b.at[r], sum_b.at[r], sum_sent.at[2 * r + 1]).wait()


def body(checkpoint, cotangent, blade_area, hub_tile, point_side, point_local):
    nx, ny = lax.axis_size("gx"), lax.axis_size("gy")
    ix, iy = lax.axis_index("gx"), lax.axis_index("gy")
    pops, rows, span = checkpoint.shape
    side = point_side.reshape(NTURB, PTS)
    tile_x = (hub_tile[:, None] // ny + side // 3 - 1) % nx
    tile_y = (hub_tile[:, None] % ny + side % 3 - 1) % ny
    mine = (tile_x == ix) & (tile_y == iy)
    cell = jnp.where(mine, point_local.reshape(NTURB, PTS), -1)
    pad = ((0, 0), (0, LANES - PTS))
    cell = jnp.pad(cell, pad, constant_values=-1)
    area = jnp.pad(blade_area.reshape(NTURB, PTS), pad)
    near = len(near_offsets(nx, REACH)) * len(near_offsets(ny, REACH)) - 1
    group, far = SUBCELLS * ny - 1, nx // SUBCELLS - 1
    f32, dma = jnp.float32, pltpu.SemaphoreType.DMA
    tile, vreg = (rows, span), (rows, LANES)
    shapes = [(STEPS, pops) + tile] + [(NTURB,) + tile] * 3 + [(NTURB,) + vreg]
    shapes += [(HALOS, 6) + vreg] * 2 + [(12,) + vreg] * 2
    shapes += [(HALOS, 4, 1, LANES)] * 2 + [(8, 1, LANES)] * 2
    shapes += [(PARTIALS, 1, LANES), (PARTIALS, near, 1, LANES)]
    shapes += [(2, 2, NTURB, LANES), (2, group, NTURB, LANES), (2, far, NTURB, LANES)]
    whole = pl.BlockSpec(memory_space=pltpu.VMEM)
    adjoint, grads = pl.pallas_call(
        functools.partial(kernel, nx, ny),
        out_shape=(jax.ShapeDtypeStruct(checkpoint.shape, f32),
                   jax.ShapeDtypeStruct((NTURB, LANES), f32)),
        in_specs=[whole] * 4,
        out_specs=(whole, whole),
        scratch_shapes=[pltpu.VMEM(shape, f32) for shape in shapes]
        + [dma((HALOS,))] * 2 + [dma((2,))] * 2 + [dma((HALOS,))] * 2 + [dma((PARTIALS,))] * 2 + [dma((4,))] * 2,
        compiler_params=pltpu.CompilerParams(
            collective_id=0, has_side_effects=True, vmem_limit_bytes=32 * 1024 * 1024),
    )(checkpoint, cotangent, area, cell)
    return adjoint, grads[:, :PTS].reshape(NTURB * PTS)


def solution(mesh):
    return jax.shard_map(
        body,
        mesh=mesh,
        in_specs=(P(None, "gx", "gy"), P(None, "gx", "gy"), P(), P(), P(), P()),
        out_specs=(P(None, "gx", "gy"), P()),
        check_vma=False,
    )
```

```python
import functools

import jax
import jax.numpy as jnp
import numpy as np
from jax import lax
from jax.experimental import pallas as pl
from jax.experimental.pallas import tpu as pltpu
from jax.sharding import PartitionSpec as P

NZ = 16
STEPS = 4
NTURB = 16
PTS = 96
LANES = 128
SUBCELLS = 4

TAU_ZERO = 0.52
SMAGORINSKY = 0.17 * 0.17
TINY = 1e-10
THRUST = 4.0
GHOST_RATES = np.array([1.05, 1.15, 1.25, 1.35, 1.45, 1.55, 1.65, 1.75, 1.85])
MESH = pl.DeviceIdType.MESH


def lattice():
    axis_part = [(1, 0, 0), (-1, 0, 0), (0, 1, 0), (0, -1, 0), (0, 0, 1), (0, 0, -1)]
    edge_part = [
        (1, 1, 0),
        (-1, -1, 0),
        (1, -1, 0),
        (-1, 1, 0),
        (1, 0, 1),
        (-1, 0, -1),
        (1, 0, -1),
        (-1, 0, 1),
        (0, 1, 1),
        (0, -1, -1),
        (0, 1, -1),
        (0, -1, 1),
    ]
    vectors = np.array([(0, 0, 0)] + axis_part + edge_part) * 1.0
    weights = np.array([1.0 / 3.0] + [1.0 / 18.0] * 6 + [1.0 / 36.0] * 12)
    opposite = np.array(
        [int(np.argmin(np.abs(vectors + vectors[column]).sum(1))) for column in range(19)]
    )
    return (vectors, weights, opposite)


def orthonormal(monomials, weights):
    rows = []
    for entry in monomials:
        vector = entry * 1.0
        for sweep in range(2):
            for other in rows:
                vector = vector - np.sum(weights * vector * other) * other
        vector = vector / np.sqrt(np.sum(weights * vector * vector))
        rows.append(vector)
    return np.stack(rows, 0)


def basis_table():
    vectors, weights, opposite = lattice()
    x, y, z = (vectors[:, 0], vectors[:, 1], vectors[:, 2])
    monomials = [np.ones(19), x, y, z, x * x, y * y, z * z, x * y, x * z, y * z]
    monomials += [x * y * y, x * z * z, y * x * x, y * z * z, z * x * x, z * y * y]
    monomials += [x * x * y * y, x * x * z * z, y * y * z * z]
    return orthonormal(monomials, weights)


VECTORS, WEIGHTS, OPPOSITE = lattice()
BASIS = basis_table()
VEC = [tuple(int(c) for c in row) for row in VECTORS]
INDEX = {vec: i for i, vec in enumerate(VEC)}
OPP = [int(i) for i in OPPOSITE]
PUSH = [float(p) for p in 3.0 * WEIGHTS * VECTORS[:, 0]]


def moving(axis, sign):
    return [i for i in range(19) if VEC[i][axis] == sign]


def total(values):
    values = list(values)
    while len(values) > 1:
        pairs = [values[k] + values[k + 1] for k in range(0, len(values) - 1, 2)]
        values = pairs + values[len(values) - len(values) % 2 :]
    return values[0]


def weighted(coefs, values):
    return total([float(c) * v for c, v in zip(coefs, values) if abs(c) > 1e-9])


def density_of(f):
    return total(f)


def momentum_of(f, axis):
    return total(f[i] for i in moving(axis, 1)) - total(f[i] for i in moving(axis, -1))


def collide(*f):
    rho = density_of(f)
    mom = [momentum_of(f, a) for a in range(3)]
    inv = 1.0 / rho
    even = {0: f[0]}
    planes = [(0, 1), (0, 2), (1, 2)]
    unit = np.eye(3, dtype=int)
    diff, cross = {}, {}
    for a in range(3):
        p = INDEX[tuple(unit[a])]
        even[a + 1] = f[p] + f[OPP[p]]
        diff[(a,)] = f[p] - f[OPP[p]]
    for k, (a, b) in enumerate(planes):
        p, q = INDEX[tuple(unit[a] + unit[b])], INDEX[tuple(unit[a] - unit[b])]
        sp, sq = f[p] + f[OPP[p]], f[q] + f[OPP[q]]
        dp, dq = f[p] - f[OPP[p]], f[q] - f[OPP[q]]
        even[4 + k] = sp + sq
        cross[k] = sp - sq
        diff[(a, b)] = dp + dq
        diff[(b, a)] = dp - dq
    stress = []
    for a in range(3):
        near = [4 + k for k, pl_ in enumerate(planes) if a in pl_]
        second = even[a + 1] + even[near[0]] + even[near[1]]
        stress.append(second - rho * (1.0 / 3.0) - mom[a] * mom[a] * inv)
    for k, (a, b) in enumerate(planes):
        stress.append(cross[k] - mom[a] * mom[b] * inv)
    square = total([p * p for p in stress[:3]]) + 2.0 * total([p * p for p in stress[3:]])
    tau = 0.5 * (
        TAU_ZERO
        + jnp.sqrt(TAU_ZERO * TAU_ZERO + 18.0 * SMAGORINSKY * jnp.sqrt(square + TINY) * inv)
    )
    rate = 1.0 / tau
    relaxed = [p * rate for p in stress]
    trace = (relaxed[0] + relaxed[1] + relaxed[2]) * (1.0 / 3.0)
    members = [0] + [INDEX[tuple(unit[a])] for a in range(3)]
    members += [INDEX[tuple(unit[a] + unit[b])] for a, b in planes]
    ghosts = [weighted(BASIS[r][members], [even[c] for c in range(7)]) for r in (16, 17, 18)]
    drop_even = []
    for c, m in enumerate(members):
        part = weighted([WEIGHTS[m] * GHOST_RATES[r - 10] * BASIS[r][m] for r in (16, 17, 18)], ghosts)
        if c == 0:
            aniso = -trace
        elif c < 4:
            aniso = relaxed[c - 1] - trace
        else:
            a, b = planes[c - 4]
            aniso = relaxed[a] + relaxed[b] - trace
        drop_even.append(part + float(4.5 * WEIGHTS[m]) * aniso)
    drop_odd = {}
    for a in range(3):
        others = [b for b in range(3) if b != a]
        kinds = [(a,)] + [(a, b) for b in others]
        reps = [INDEX[tuple(unit[a])]] + [INDEX[tuple(unit[a] + unit[b])] for b in others]
        rows = (10 + 2 * a, 11 + 2 * a)
        odd = [weighted(BASIS[r][reps], [diff[k] for k in kinds]) for r in rows]
        for kind, m in zip(kinds, reps):
            drop_odd[kind] = weighted([WEIGHTS[m] * GHOST_RATES[r - 10] * BASIS[r][m] for r in rows], odd)
    out = [None] * 19
    out[0] = f[0] - drop_even[0]
    for a in range(3):
        p = INDEX[tuple(unit[a])]
        out[p] = f[p] - (drop_even[a + 1] + drop_odd[(a,)])
        out[OPP[p]] = f[OPP[p]] - (drop_even[a + 1] - drop_odd[(a,)])
    for k, (a, b) in enumerate(planes):
        p, q = INDEX[tuple(unit[a] + unit[b])], INDEX[tuple(unit[a] - unit[b])]
        shear = 0.25 * relaxed[3 + k]
        plus, minus = drop_even[4 + k] + shear, drop_even[4 + k] - shear
        odd_p = drop_odd[(a, b)] + drop_odd[(b, a)]
        odd_q = drop_odd[(a, b)] - drop_odd[(b, a)]
        out[p] = f[p] - (plus + odd_p)
        out[OPP[p]] = f[OPP[p]] - (plus - odd_p)
        out[q] = f[q] - (minus + odd_q)
        out[OPP[q]] = f[OPP[q]] - (minus - odd_q)
    return tuple(out)


RIMS = [(1, 0, 0, 2), (-1, 0, 2, 2), (0, 1, 4, 1), (0, -1, 5, 1)]
CORNERS = [(1, 1, 0, 1), (1, -1, 1, 1), (-1, 1, 2, 1), (-1, -1, 3, 1)]
CORNER = {(dx, dy): slot for dx, dy, slot, count in CORNERS}
SIDES = [(dx, dy) for dy in (1, -1) for dx in (0, 1, -1)]
REACH = 3
HALOS = 2 * STEPS
PARTIALS = 2 * STEPS - 1


def near_offsets(size, reach):
    return sorted({d % size for d in range(-reach, reach + 1)})


def merged(rims, nx, ny):
    copies = []
    for dx, dy, slot, count in rims:
        where = (dx % nx, dy % ny)
        if copies and copies[-1][0] == where:
            copies[-1] = (where, copies[-1][1], copies[-1][2] + count)
        else:
            copies.append((where, slot, count))
    return copies


def thirds(value):
    high = value.astype(jnp.bfloat16).astype(jnp.float32)
    rest = value - high
    middle = rest.astype(jnp.bfloat16).astype(jnp.float32)
    parts = [high, middle, rest - middle, jnp.zeros_like(value)]
    return jnp.concatenate(parts, axis=0).astype(jnp.bfloat16)


def join_thirds(product):
    rows = product.shape[0] // 4
    return product[:rows] + (product[rows : 2 * rows] + product[2 * rows : 3 * rows])


def kernel(nx, ny, start_hbm, cotangent_hbm, hubs_hbm, area_hbm, side_hbm, local_hbm, grad, area_grad,
           checkpoint, cotangent, hubs, flat_area, flat_side, flat_local, area, cell, flats, spread, grads,
           ext_x, ext_y, halo_out, halo_in, rim_out, rim_in, turn_out, turn_in, rim_turn_out, rim_turn_in, part_out, part_in, sum_out, sum_a, sum_b,
           halo_sent, halo_got, rim_sent, rim_got, turn_sent, turn_got, part_sent, part_got, sum_sent, sum_got, loaded):
    ix, iy = lax.axis_index("gx"), lax.axis_index("gy")
    near = [(dx, dy) for dx in near_offsets(nx, REACH) for dy in near_offsets(ny, REACH)]
    near = [o for o in near if o != (0, 0)]
    near.sort(key=lambda o: (-min(o[0], nx - o[0]), -min(o[1], ny - o[1])))
    low = SUBCELLS
    group = [(a, b) for a in range(low) for b in range(ny) if (a, b) != (0, 0)]
    far = list(range(1, nx // low))

    def at(dx, dy):
        return (lax.rem(ix + dx, nx), lax.rem(iy + dy, ny))

    base = lax.rem(ix, low)

    def in_group(a, b):
        return (ix - base + lax.rem(base + a, low), lax.rem(iy + b, ny))

    def in_far(c):
        return (lax.rem(ix + low * c, nx), iy)

    targets = [at(*o) for o in near] + [in_group(*o) for o in group] + [in_far(c) for c in far]
    barrier = pltpu.get_barrier_semaphore()
    for target in targets:
        pl.semaphore_signal(barrier, inc=1, device_id=target, device_id_type=MESH)

    sources = [start_hbm, hubs_hbm, side_hbm, local_hbm, area_hbm, cotangent_hbm]
    places = [checkpoint, hubs, flat_side, flat_local, flat_area, cotangent]
    loads = [pltpu.make_async_copy(src, dst, loaded.at[k]) for k, (src, dst) in enumerate(zip(sources, places))]
    for load in loads:
        load.start()

    rows, span = checkpoint.shape[1:]
    half = span - LANES
    row = lax.broadcasted_iota(jnp.int32, (rows, span), 0)
    lane = lax.broadcasted_iota(jnp.int32, (rows, span), 1)
    z = lax.bitwise_and(lane, NZ - 1)
    first_z, last_z = z == 0, z == NZ - 1
    row_h = lax.broadcasted_iota(jnp.int32, (rows, LANES), 0)
    lane_h = lax.broadcasted_iota(jnp.int32, (rows, LANES), 1)
    slot_h = lax.shift_right_logical(lane_h, 4)
    row_t = lax.broadcasted_iota(jnp.int32, (NTURB, LANES), 0)
    lane_t = lax.broadcasted_iota(jnp.int32, (NTURB, LANES), 1)

    def turned(value, shift, axis):
        shift = shift % value.shape[axis]
        return pltpu.roll(value, shift, axis) if shift else value

    def edge_of(sign):
        return rows - 1 if sign == 1 else 0

    def rim_lane(sign):
        return LANES - NZ if sign == 1 else 0

    def side_of(value, sign):
        return value[:, half:] if sign == 1 else value[:, :LANES]

    def pack_x(values, sign):
        packed = jnp.zeros((rows, span), jnp.float32)
        for k, value in enumerate(values):
            packed = jnp.where(row == k, turned(value, k - edge_of(sign), 0), packed)
        return packed

    def pack_y(values, sign):
        packed = jnp.zeros((rows, LANES), jnp.float32)
        for k, value in enumerate(values):
            moved = turned(side_of(value, sign), NZ * k - rim_lane(sign), 1)
            packed = jnp.where(slot_h == k, moved, packed)
        return packed

    def send_halo(f, fields, e, greeted=None):
        for sign, start in ((1, 0), (-1, 2)):
            packed = pack_x([f[i] for i in moving(0, sign)] + fields, sign)
            halo_out[e, start] = packed[:, :LANES]
            halo_out[e, start + 1] = packed[:, half:]
        for sign, start in ((1, 4), (-1, 5)):
            halo_out[e, start] = pack_y([f[i] for i in moving(1, sign)] + fields, sign)
            for dx in (1, -1):
                edge = edge_of(dx)
                turn_out[e, CORNER[(dx, sign)]] = halo_out[e, start, edge : edge + 1]
        if greeted is not None:
            pl.semaphore_wait(barrier, greeted)
        send_rims(halo_out.at[e], halo_in.at[e], turn_out.at[e], turn_in.at[e], 1,
                  (halo_sent.at[e], halo_got.at[e], turn_sent.at[e], turn_got.at[e]))

    def send_rims(out, into, turn, into_turn, scale, sems):
        for rims, source, target, sent, got in ((RIMS, out, into) + sems[:2], (CORNERS, turn, into_turn) + sems[2:]):
            for where, slot, count in merged(rims, nx, ny):
                part = pl.ds(scale * slot, scale * count)
                pltpu.make_async_remote_copy(
                    src_ref=source.at[part], dst_ref=target.at[part], send_sem=sent, recv_sem=got,
                    device_id=at(*where), device_id_type=MESH).start()

    def receive(e, count):
        pltpu.make_async_copy(halo_in.at[e], halo_in.at[e], halo_got.at[e]).wait()
        pltpu.make_async_copy(turn_in.at[e], turn_in.at[e], turn_got.at[e]).wait()
        from_x, from_y = {}, {}
        fields_x = [None] * count
        fields_y = [jnp.zeros((rows, LANES), jnp.float32)] * count
        for sign, start in ((1, 0), (-1, 2)):
            got = jnp.concatenate([halo_in[e, start], halo_in[e, start + 1]], axis=1)
            for k, i in enumerate(moving(0, sign)):
                from_x[i] = turned(got, edge_of(sign) - k, 0)
            for k in range(count):
                value = turned(got, edge_of(sign) - 5 - k, 0)
                fields_x[k] = value if sign == 1 else jnp.where(row == 0, value, fields_x[k])
        for side, (dx, dy) in enumerate(SIDES):
            got = halo_in[e, 4 if dy == 1 else 5]
            if dx:
                got = jnp.where(row_h == edge_of(dx), turn_in[e, CORNER[(dx, dy)]], got)
            for k, i in enumerate(moving(1, dy)):
                if VEC[i][0] == dx:
                    from_y[i] = turned(got, rim_lane(dy) - NZ * k, 1)
            for k in range(count):
                value = turned(got, NZ * (side - 5 - k), 1)
                fields_y[k] = jnp.where(slot_h == side, value, fields_y[k])
        return from_x, from_y, fields_x, fields_y

    def run(f, from_x, from_y):
        out = {}
        for i in f:
            dx, dy, dz = VEC[i]
            value = f[i]
            if dx:
                value = jnp.where(row == edge_of(dx), from_x[i], value)
            if dy == 1:
                edge = jnp.where(lane_h >= LANES - NZ, from_y[i], value[:, half:])
                value = jnp.concatenate([value[:, :half], edge], axis=1)
            elif dy == -1:
                edge = jnp.where(lane_h < NZ, from_y[i], value[:, :LANES])
                value = jnp.concatenate([edge, value[:, LANES:]], axis=1)
            value = turned(turned(value, dx, 0), NZ * dy + dz, 1)
            if dz:
                value = jnp.where(first_z if dz == 1 else last_z, f[OPP[i]], value)
            out[i] = value
        return out

    def pulls_of(rate):
        lines = [jnp.broadcast_to(rate[t : t + 1], (rows, LANES)) for t in range(NTURB)]
        wides = [jnp.concatenate([line] * (span // LANES), axis=1) for line in lines]
        return (total([spread[t] * wides[t] for t in range(NTURB)]),
                total([ext_x[t] * wides[t] for t in range(NTURB)]),
                total([ext_y[t] * lines[t] for t in range(NTURB)]))

    def run_added(entries, correct, fields, fields_x, fields_y, pulls):
        add = correct(fields, [p[0] for p in pulls])
        add_x = correct(fields_x, [p[1] for p in pulls])
        add_y = correct(fields_y, [p[2] for p in pulls])
        from_x = {i: add_x(i) for i in entries if VEC[i][0]}
        from_y = {}
        for side, (dx, dy) in enumerate(SIDES):
            inside = [i for i in entries if VEC[i][:2] == (dx, dy)]
            if inside:
                value = turned(add_y(inside[0]), rim_lane(dy) - NZ * side, 1)
                from_y.update({i: value for i in inside})
        return run({i: add(i) for i in entries}, from_x, from_y)

    def turbine_sums(value):
        sums = []
        for t in range(NTURB):
            prod = spread[t] * value
            sums.append(jnp.sum(prod[:, :LANES] + prod[:, half:], axis=0, keepdims=True))
        sums = jnp.sum(jnp.concatenate(sums, axis=0), axis=1, keepdims=True)
        return jnp.broadcast_to(sums, (NTURB, LANES))

    def send_partials(sums, e):
        width = LANES // (NTURB * len(sums))
        packed = jnp.zeros((NTURB, LANES), jnp.float32)
        for c, value in enumerate(sums):
            packed = jnp.where(lane_t // width == row_t + NTURB * c, value, packed)
        part_out[e] = jnp.sum(packed, axis=0, keepdims=True)
        for k, (dx, dy) in enumerate(near):
            pltpu.make_async_remote_copy(
                src_ref=part_out.at[e], dst_ref=part_in.at[e, k],
                send_sem=part_sent.at[e], recv_sem=part_got.at[e],
                device_id=at(dx, dy), device_id_type=MESH).start()

    def take_partials(count, e):
        width = LANES // (NTURB * count)
        pltpu.make_async_copy(part_in.at[e], part_in.at[e], part_got.at[e]).wait()
        both = total([part_out[e]] + [part_in[e, k] for k in range(len(near))])
        both = jnp.broadcast_to(both, (NTURB, LANES))
        out = []
        for c in range(count):
            picked = jnp.where(lane_t == width * (row_t + NTURB * c), both, 0.0)
            line = jnp.sum(picked, axis=1, keepdims=True)
            out.append(jnp.broadcast_to(line, (NTURB, LANES)) / denom)
        return out

    def wide(value, t):
        line = jnp.broadcast_to(value[t : t + 1], (rows, LANES))
        return jnp.concatenate([line] * (span // LANES), axis=1)

    def onehots(t):
        index = cell[t : t + 1, :]
        across = lax.shift_right_arithmetic(index, 8)
        along = lax.bitwise_and(index, 255)
        pick_x = lax.broadcasted_iota(jnp.int32, (rows, LANES), 0) == across
        pick_j = lax.broadcasted_iota(jnp.int32, (span, LANES), 0) == along
        return pick_x, jnp.where(pick_j, 1.0, 0.0).astype(jnp.bfloat16)

    def at_points(fields):
        lines = []
        for t in range(NTURB):
            pick_x, pick_j = onehots(t)
            found = join_thirds(jnp.dot(thirds(fields(t)), pick_j, preferred_element_type=jnp.float32))
            lines.append(jnp.sum(jnp.where(pick_x, found, 0.0), axis=0, keepdims=True))
        return jnp.concatenate(lines, axis=0)

    def sum_first(value, r):
        sum_out[r, 0] = value
        for k, (a, b) in enumerate(group):
            pltpu.make_async_remote_copy(
                src_ref=sum_out.at[r, 0], dst_ref=sum_a.at[r, k], send_sem=sum_sent.at[2 * r],
                recv_sem=sum_got.at[2 * r], device_id=in_group(a, b), device_id_type=MESH).start()

    def sum_second(r):
        pltpu.make_async_copy(sum_a.at[r], sum_a.at[r], sum_got.at[2 * r]).wait()
        sum_out[r, 1] = total([sum_out[r, 0]] + [sum_a[r, k] for k in range(len(group))])
        for k, c in enumerate(far):
            pltpu.make_async_remote_copy(
                src_ref=sum_out.at[r, 1], dst_ref=sum_b.at[r, k], send_sem=sum_sent.at[2 * r + 1],
                recv_sem=sum_got.at[2 * r + 1], device_id=in_far(c), device_id_type=MESH).start()

    def sum_last(r):
        pltpu.make_async_copy(sum_b.at[r], sum_b.at[r], sum_got.at[2 * r + 1]).wait()
        return total([sum_out[r, 1]] + [sum_b[r, k] for k in range(len(far))])

    loads[0].wait()
    field = [checkpoint[i] for i in range(19)]
    send_halo(field, [], 0, len(targets))

    def by_turbine(value):
        lines = []
        for t in range(NTURB):
            line, first = divmod(PTS * t, LANES)
            here = value[line : line + 1]
            if first + PTS > LANES:
                here = jnp.where(lane_t[:1] >= first, here, value[line + 1 : line + 2])
            lines.append(turned(here, -first, 1))
        return jnp.concatenate(lines, axis=0)

    def in_a_row(value):
        lines = []
        for line in range(NTURB * PTS // LANES):
            t, first = divmod(LANES * line, PTS)
            count = PTS - first
            after = turned(value[t + 1 : t + 2], count, 1)
            lines.append(jnp.where(lane_t[:1] < count, turned(value[t : t + 1], -first, 1), after))
        return jnp.concatenate(lines, axis=0)

    for load in loads[1:5]:
        load.wait()
    code = by_turbine(flat_side[...] * (rows * span) + flat_local[...])
    side = lax.shift_right_logical(code, 11)
    side_x = jnp.where(side >= 6, 2, jnp.where(side >= 3, 1, 0))
    side_y = side - 3 * side_x
    off_x, off_y = side_x - 1, side_y - 1
    hub_x, hub_y = jnp.zeros_like(side), jnp.zeros_like(side)
    for t in range(NTURB):
        hub = hubs[t]
        hub_x = jnp.where(row_t == t, lax.div(hub, ny) - ix, hub_x)
        hub_y = jnp.where(row_t == t, lax.rem(hub, ny) - iy, hub_y)
    off_x, off_y = off_x + hub_x, off_y + hub_y
    mine = (off_x == 0) | (off_x == nx) | (off_x == -nx)
    mine = mine & ((off_y == 0) | (off_y == ny) | (off_y == -ny)) & (lane_t < PTS)
    cell[...] = jnp.where(mine, lax.bitwise_and(code, rows * span - 1), -1)
    area[...] = jnp.where(lane_t < PTS, by_turbine(flat_area[...]), 0.0)

    for t in range(NTURB):
        pick_x, pick_j = onehots(t)
        weight = jnp.where(pick_x, area[t : t + 1, :], 0.0)
        spread[t] = join_thirds(lax.dot_general(
            thirds(weight), pick_j, (((1,), (1,)), ((), ())), preferred_element_type=jnp.float32))
    denom = jnp.broadcast_to(jnp.sum(area[...], axis=1, keepdims=True), (NTURB, LANES))
    for h in range(2):
        mine = [spread[8 * h + k] for k in range(8)]
        for sign, start in ((1, 0), (-1, 4)):
            packed = pack_x(mine, sign)
            rim_out[start + 2 * h] = packed[:, :LANES]
            rim_out[start + 2 * h + 1] = packed[:, half:]
        for sign, start in ((1, 8), (-1, 10)):
            rim_out[start + h] = pack_y(mine, sign)
    for sign, start in ((1, 8), (-1, 10)):
        for dx in (1, -1):
            for h in range(2):
                edge = edge_of(dx)
                rim_turn_out[2 * CORNER[(dx, sign)] + h] = rim_out[start + h, edge : edge + 1]
    send_rims(rim_out, rim_in, rim_turn_out, rim_turn_in, 2,
              (rim_sent.at[0], rim_got.at[0], rim_sent.at[1], rim_got.at[1]))

    def extend_spread():
        pltpu.make_async_copy(rim_in, rim_in, rim_got.at[0]).wait()
        pltpu.make_async_copy(rim_turn_in, rim_turn_in, rim_got.at[1]).wait()
        sides = []
        for dx, dy in SIDES:
            pair = []
            for h in range(2):
                value = rim_in[(8 if dy == 1 else 10) + h]
                if dx:
                    corner = rim_turn_in[2 * CORNER[(dx, dy)] + h]
                    value = jnp.where(row_h == edge_of(dx), corner, value)
                pair.append(value)
            sides.append(pair)
        for h in range(2):
            ups = jnp.concatenate([rim_in[2 * h], rim_in[2 * h + 1]], axis=1)
            downs = jnp.concatenate([rim_in[4 + 2 * h], rim_in[5 + 2 * h]], axis=1)
            for k in range(8):
                up, down = turned(ups, rows - 1 - k, 0), turned(downs, -k, 0)
                ext_x[8 * h + k] = jnp.where(row == rows - 1, up, jnp.where(row == 0, down, 0.0))
                packed = jnp.zeros((rows, LANES), jnp.float32)
                for side, pair in enumerate(sides):
                    moved = turned(pair[h], NZ * (side - k), 1)
                    packed = jnp.where(slot_h == side, moved, packed)
                ext_y[8 * h + k] = packed

    def forced(fields, pulls):
        force = -THRUST * fields[0] * pulls[0]
        return lambda i: PUSH[i] * force

    def speed_fixed(fields, pulls):
        speed_bar = fields[1] * pulls[0] + fields[2] * pulls[1]
        parts = {c: (float(-c) - fields[0]) * speed_bar for c in (-1, 0, 1)}
        return lambda i: parts[VEC[i][0]]

    rotors, speeds, pulls = [], [], []
    from_x, from_y, unused_x, unused_y = receive(0, 0)
    flat = run(dict(enumerate(field)), from_x, from_y)
    pushed_on = [i for i in range(19) if PUSH[i] != 0.0]
    for s in range(STEPS):
        flat = [flat[i] for i in range(19)]
        for i in range(19):
            flats[s, i] = flat[i]
        speed = momentum_of(flat, 0) / density_of(flat)
        speeds.append(speed)
        if s == STEPS - 1:
            break
        send_partials([turbine_sums(speed)], s)
        moved = collide(*flat)
        send_halo(moved, [speed], s + 1)
        if s == 0:
            extend_spread()
        from_x, from_y, fields_x, fields_y = receive(s + 1, 1)
        flat = run(dict(enumerate(moved)), from_x, from_y)
        rotors.append(take_partials(1, s)[0])
        pulls.append(pulls_of(rotors[s]))
        added = run_added(pushed_on, forced, [speed], fields_x, fields_y, [pulls[s]])
        flat.update({i: flat[i] + added[i] for i in pushed_on})

    loads[5].wait()
    adjoint = [cotangent[i] for i in range(19)]
    for n in range(STEPS):
        s, e = STEPS - 1 - n, STEPS + n
        flat = [flats[s, i] for i in range(19)]
        speed = speeds[s]
        force_bar = weighted(PUSH, adjoint)
        load = -THRUST * force_bar * speed
        load_sums = turbine_sums(load)
        if n == 0:
            send_partials([turbine_sums(speed), load_sums], s)
        else:
            send_partials([load_sums], s + 2 * n)
        if n == STEPS - 1:
            rotor = rotors[s]
            found = at_points(lambda t: grads[t] + wide(rotor, t) * load)
            sum_first(jnp.where(lane_t < PTS, found, load_sums), 1)
        unused, pullback = jax.vjp(collide, *flat)
        flat_bar = pullback(tuple(adjoint))
        inverse = 1.0 / density_of(flat)
        fields = [speed, inverse, -THRUST * force_bar * inverse]
        turned_bar = [flat_bar[OPP[i]] for i in range(19)]
        send_halo(turned_bar, fields, e)
        if n == 0:
            sum_first(at_points(lambda t: speeds[0] - wide(rotors[0], t)), 0)
        elif n == 1:
            sum_second(0)
        if n == STEPS - 1:
            sum_second(1)
        from_x, from_y, fields_x, fields_y = receive(e, 3)
        pushed = run(dict(enumerate(turned_bar)), from_x, from_y)
        if n == 0:
            rotor, numer_bar = take_partials(2, s)
            pulls.append(pulls_of(rotor))
        else:
            rotor = rotors[s]
            numer_bar = take_partials(1, s + 2 * n)[0]
        added = run_added(range(19), speed_fixed, fields, fields_x, fields_y, [pulls_of(numer_bar), pulls[s]])
        adjoint = [pushed[OPP[i]] + added[OPP[i]] for i in range(19)]
        if n < STEPS - 1:
            for t in range(NTURB):
                turn = wide(rotor, t)
                part = turn * load + wide(numer_bar, t) * (speed - turn)
                grads[t] = part if n == 0 else grads[t] + part

    for i in range(19):
        grad[i] = adjoint[i]
    spread_of = sum_last(0)
    sums = sum_last(1)
    numer_bar = jnp.broadcast_to(sums[:, PTS : PTS + 1], (NTURB, LANES)) / denom
    area_grad[...] = in_a_row(sums + numer_bar * spread_of)

    for e in range(HALOS):
        pltpu.make_async_copy(halo_in.at[e], halo_in.at[e], halo_sent.at[e]).wait()
        pltpu.make_async_copy(turn_in.at[e], turn_in.at[e], turn_sent.at[e]).wait()
    for e in range(PARTIALS):
        pltpu.make_async_copy(part_in.at[e], part_in.at[e], part_sent.at[e]).wait()
    pltpu.make_async_copy(rim_in, rim_in, rim_sent.at[0]).wait()
    pltpu.make_async_copy(rim_turn_in, rim_turn_in, rim_sent.at[1]).wait()
    for r in range(2):
        pltpu.make_async_copy(sum_a.at[r], sum_a.at[r], sum_sent.at[2 * r]).wait()
        pltpu.make_async_copy(sum_b.at[r], sum_b.at[r], sum_sent.at[2 * r + 1]).wait()


def body(checkpoint, cotangent, blade_area, hub_tile, point_side, point_local):
    nx, ny = lax.axis_size("gx"), lax.axis_size("gy")
    pops, rows, span = checkpoint.shape
    lines = (NTURB * PTS // LANES, LANES)
    near = len(near_offsets(nx, REACH)) * len(near_offsets(ny, REACH)) - 1
    group, far = SUBCELLS * ny - 1, nx // SUBCELLS - 1
    f32, dma = jnp.float32, pltpu.SemaphoreType.DMA
    tile, vreg = (rows, span), (rows, LANES)
    ints = [pltpu.SMEM((NTURB,), jnp.int32), pltpu.VMEM(lines, f32)]
    ints += [pltpu.VMEM(lines, jnp.int32)] * 2
    ints += [pltpu.VMEM((NTURB, LANES), f32), pltpu.VMEM((NTURB, LANES), jnp.int32)]
    shapes = [(STEPS, pops) + tile] + [(NTURB,) + tile] * 3 + [(NTURB,) + vreg]
    shapes += [(HALOS, 6) + vreg] * 2 + [(12,) + vreg] * 2
    shapes += [(HALOS, 4, 1, LANES)] * 2 + [(8, 1, LANES)] * 2
    shapes += [(PARTIALS, 1, LANES), (PARTIALS, near, 1, LANES)]
    shapes += [(2, 2, NTURB, LANES), (2, group, NTURB, LANES), (2, far, NTURB, LANES)]
    whole = pl.BlockSpec(memory_space=pltpu.VMEM)
    adjoint, grads = pl.pallas_call(
        functools.partial(kernel, nx, ny),
        out_shape=(jax.ShapeDtypeStruct(checkpoint.shape, f32),
                   jax.ShapeDtypeStruct(lines, f32)),
        in_specs=[pl.BlockSpec(memory_space=pltpu.HBM)] * 6,
        out_specs=(whole, whole),
        scratch_shapes=[pltpu.VMEM((pops,) + tile, f32)] * 2 + ints
        + [pltpu.VMEM(shape, f32) for shape in shapes]
        + [dma((HALOS,))] * 2 + [dma((2,))] * 2 + [dma((HALOS,))] * 2 + [dma((PARTIALS,))] * 2 + [dma((4,))] * 2 + [dma((6,))],
        compiler_params=pltpu.CompilerParams(
            collective_id=0, has_side_effects=True, vmem_limit_bytes=60 * 1024 * 1024),
    )(checkpoint, cotangent, hub_tile, blade_area.reshape(lines), point_side.reshape(lines), point_local.reshape(lines))
    return adjoint, grads.reshape(NTURB * PTS)


def solution(mesh):
    return jax.shard_map(
        body,
        mesh=mesh,
        in_specs=(P(None, "gx", "gy"), P(None, "gx", "gy"), P(), P(), P(), P()),
        out_specs=(P(None, "gx", "gy"), P()),
        check_vma=False,
    )
```

```python
import functools

import jax
import jax.numpy as jnp
import numpy as np
from jax import lax
from jax.experimental import pallas as pl
from jax.experimental.pallas import tpu as pltpu
from jax.sharding import PartitionSpec as P

NZ = 16
STEPS = 4
NTURB = 16
PTS = 96
LANES = 128
SUBCELLS = 4

TAU_ZERO = 0.52
SMAGORINSKY = 0.17 * 0.17
TINY = 1e-10
THRUST = 4.0
GHOST_RATES = np.array([1.05, 1.15, 1.25, 1.35, 1.45, 1.55, 1.65, 1.75, 1.85])
MESH = pl.DeviceIdType.MESH


def lattice():
    axis_part = [(1, 0, 0), (-1, 0, 0), (0, 1, 0), (0, -1, 0), (0, 0, 1), (0, 0, -1)]
    edge_part = [
        (1, 1, 0),
        (-1, -1, 0),
        (1, -1, 0),
        (-1, 1, 0),
        (1, 0, 1),
        (-1, 0, -1),
        (1, 0, -1),
        (-1, 0, 1),
        (0, 1, 1),
        (0, -1, -1),
        (0, 1, -1),
        (0, -1, 1),
    ]
    vectors = np.array([(0, 0, 0)] + axis_part + edge_part) * 1.0
    weights = np.array([1.0 / 3.0] + [1.0 / 18.0] * 6 + [1.0 / 36.0] * 12)
    opposite = np.array(
        [int(np.argmin(np.abs(vectors + vectors[column]).sum(1))) for column in range(19)]
    )
    return (vectors, weights, opposite)


def orthonormal(monomials, weights):
    rows = []
    for entry in monomials:
        vector = entry * 1.0
        for sweep in range(2):
            for other in rows:
                vector = vector - np.sum(weights * vector * other) * other
        vector = vector / np.sqrt(np.sum(weights * vector * vector))
        rows.append(vector)
    return np.stack(rows, 0)


def basis_table():
    vectors, weights, opposite = lattice()
    x, y, z = (vectors[:, 0], vectors[:, 1], vectors[:, 2])
    monomials = [np.ones(19), x, y, z, x * x, y * y, z * z, x * y, x * z, y * z]
    monomials += [x * y * y, x * z * z, y * x * x, y * z * z, z * x * x, z * y * y]
    monomials += [x * x * y * y, x * x * z * z, y * y * z * z]
    return orthonormal(monomials, weights)


VECTORS, WEIGHTS, OPPOSITE = lattice()
BASIS = basis_table()
VEC = [tuple(int(c) for c in row) for row in VECTORS]
INDEX = {vec: i for i, vec in enumerate(VEC)}
OPP = [int(i) for i in OPPOSITE]
PUSH = [float(p) for p in 3.0 * WEIGHTS * VECTORS[:, 0]]


def moving(axis, sign):
    return [i for i in range(19) if VEC[i][axis] == sign]


def total(values):
    values = list(values)
    while len(values) > 1:
        pairs = [values[k] + values[k + 1] for k in range(0, len(values) - 1, 2)]
        values = pairs + values[len(values) - len(values) % 2 :]
    return values[0]


def weighted(coefs, values):
    return total([float(c) * v for c, v in zip(coefs, values) if abs(c) > 1e-9])


def density_of(f):
    return total(f)


def momentum_of(f, axis):
    return total(f[i] for i in moving(axis, 1)) - total(f[i] for i in moving(axis, -1))


def collide(*f):
    rho = density_of(f)
    mom = [momentum_of(f, a) for a in range(3)]
    inv = 1.0 / rho
    even = {0: f[0]}
    planes = [(0, 1), (0, 2), (1, 2)]
    unit = np.eye(3, dtype=int)
    diff, cross = {}, {}
    for a in range(3):
        p = INDEX[tuple(unit[a])]
        even[a + 1] = f[p] + f[OPP[p]]
        diff[(a,)] = f[p] - f[OPP[p]]
    for k, (a, b) in enumerate(planes):
        p, q = INDEX[tuple(unit[a] + unit[b])], INDEX[tuple(unit[a] - unit[b])]
        sp, sq = f[p] + f[OPP[p]], f[q] + f[OPP[q]]
        dp, dq = f[p] - f[OPP[p]], f[q] - f[OPP[q]]
        even[4 + k] = sp + sq
        cross[k] = sp - sq
        diff[(a, b)] = dp + dq
        diff[(b, a)] = dp - dq
    stress = []
    for a in range(3):
        near = [4 + k for k, pl_ in enumerate(planes) if a in pl_]
        second = even[a + 1] + even[near[0]] + even[near[1]]
        stress.append(second - rho * (1.0 / 3.0) - mom[a] * mom[a] * inv)
    for k, (a, b) in enumerate(planes):
        stress.append(cross[k] - mom[a] * mom[b] * inv)
    square = total([p * p for p in stress[:3]]) + 2.0 * total([p * p for p in stress[3:]])
    tau = 0.5 * (
        TAU_ZERO
        + jnp.sqrt(TAU_ZERO * TAU_ZERO + 18.0 * SMAGORINSKY * jnp.sqrt(square + TINY) * inv)
    )
    rate = 1.0 / tau
    relaxed = [p * rate for p in stress]
    trace = (relaxed[0] + relaxed[1] + relaxed[2]) * (1.0 / 3.0)
    members = [0] + [INDEX[tuple(unit[a])] for a in range(3)]
    members += [INDEX[tuple(unit[a] + unit[b])] for a, b in planes]
    ghosts = [weighted(BASIS[r][members], [even[c] for c in range(7)]) for r in (16, 17, 18)]
    drop_even = []
    for c, m in enumerate(members):
        part = weighted([WEIGHTS[m] * GHOST_RATES[r - 10] * BASIS[r][m] for r in (16, 17, 18)], ghosts)
        if c == 0:
            aniso = -trace
        elif c < 4:
            aniso = relaxed[c - 1] - trace
        else:
            a, b = planes[c - 4]
            aniso = relaxed[a] + relaxed[b] - trace
        drop_even.append(part + float(4.5 * WEIGHTS[m]) * aniso)
    drop_odd = {}
    for a in range(3):
        others = [b for b in range(3) if b != a]
        kinds = [(a,)] + [(a, b) for b in others]
        reps = [INDEX[tuple(unit[a])]] + [INDEX[tuple(unit[a] + unit[b])] for b in others]
        rows = (10 + 2 * a, 11 + 2 * a)
        odd = [weighted(BASIS[r][reps], [diff[k] for k in kinds]) for r in rows]
        for kind, m in zip(kinds, reps):
            drop_odd[kind] = weighted([WEIGHTS[m] * GHOST_RATES[r - 10] * BASIS[r][m] for r in rows], odd)
    out = [None] * 19
    out[0] = f[0] - drop_even[0]
    for a in range(3):
        p = INDEX[tuple(unit[a])]
        out[p] = f[p] - (drop_even[a + 1] + drop_odd[(a,)])
        out[OPP[p]] = f[OPP[p]] - (drop_even[a + 1] - drop_odd[(a,)])
    for k, (a, b) in enumerate(planes):
        p, q = INDEX[tuple(unit[a] + unit[b])], INDEX[tuple(unit[a] - unit[b])]
        shear = 0.25 * relaxed[3 + k]
        plus, minus = drop_even[4 + k] + shear, drop_even[4 + k] - shear
        odd_p = drop_odd[(a, b)] + drop_odd[(b, a)]
        odd_q = drop_odd[(a, b)] - drop_odd[(b, a)]
        out[p] = f[p] - (plus + odd_p)
        out[OPP[p]] = f[OPP[p]] - (plus - odd_p)
        out[q] = f[q] - (minus + odd_q)
        out[OPP[q]] = f[OPP[q]] - (minus - odd_q)
    return tuple(out)


RIMS = [(1, 0, 0, 2), (-1, 0, 2, 2), (0, 1, 4, 1), (0, -1, 5, 1)]
CORNERS = [(1, 1, 0, 1), (1, -1, 1, 1), (-1, 1, 2, 1), (-1, -1, 3, 1)]
CORNER = {(dx, dy): slot for dx, dy, slot, count in CORNERS}
SIDES = [(dx, dy) for dy in (1, -1) for dx in (0, 1, -1)]
REACH = 3
HALOS = 2 * STEPS
PARTIALS = 2 * STEPS - 1


def near_offsets(size, reach):
    return sorted({d % size for d in range(-reach, reach + 1)})


def merged(rims, nx, ny):
    copies = []
    for dx, dy, slot, count in rims:
        where = (dx % nx, dy % ny)
        if copies and copies[-1][0] == where:
            copies[-1] = (where, copies[-1][1], copies[-1][2] + count)
        else:
            copies.append((where, slot, count))
    return copies


def thirds(value):
    high = value.astype(jnp.bfloat16).astype(jnp.float32)
    rest = value - high
    middle = rest.astype(jnp.bfloat16).astype(jnp.float32)
    parts = [high, middle, rest - middle, jnp.zeros_like(value)]
    return jnp.concatenate(parts, axis=0).astype(jnp.bfloat16)


def join_thirds(product):
    rows = product.shape[0] // 4
    return product[:rows] + (product[rows : 2 * rows] + product[2 * rows : 3 * rows])


def kernel(nx, ny, start_hbm, cotangent_hbm, hubs_hbm, area_hbm, side_hbm, local_hbm, grad, area_grad,
           checkpoint, cotangent, hubs, flat_area, flat_side, flat_local, area, cell, flats, spread, grads,
           ext_x, ext_y, halo_out, halo_in, rim_out, rim_in, turn_out, turn_in, rim_turn_out, rim_turn_in, part_out, part_in, sum_out, sum_a, sum_b,
           halo_sent, halo_got, rim_sent, rim_got, turn_sent, turn_got, part_sent, part_got, sum_sent, sum_got, loaded):
    ix, iy = lax.axis_index("gx"), lax.axis_index("gy")
    near = [(dx, dy) for dx in near_offsets(nx, REACH) for dy in near_offsets(ny, REACH)]
    near = [o for o in near if o != (0, 0)]
    near.sort(key=lambda o: (-min(o[0], nx - o[0]), -min(o[1], ny - o[1])))
    low = SUBCELLS
    group = [(a, b) for a in range(low) for b in range(ny) if (a, b) != (0, 0)]
    far = list(range(1, nx // low))

    def at(dx, dy):
        return (lax.rem(ix + dx, nx), lax.rem(iy + dy, ny))

    base = lax.rem(ix, low)

    def in_group(a, b):
        return (ix - base + lax.rem(base + a, low), lax.rem(iy + b, ny))

    def in_far(c):
        return (lax.rem(ix + low * c, nx), iy)

    targets = [at(*o) for o in near] + [in_group(*o) for o in group] + [in_far(c) for c in far]
    barrier = pltpu.get_barrier_semaphore()
    for target in targets:
        pl.semaphore_signal(barrier, inc=1, device_id=target, device_id_type=MESH)

    sources = [start_hbm, hubs_hbm, side_hbm, local_hbm, area_hbm, cotangent_hbm]
    places = [checkpoint, hubs, flat_side, flat_local, flat_area, cotangent]
    loads = [pltpu.make_async_copy(src, dst, loaded.at[k]) for k, (src, dst) in enumerate(zip(sources, places))]
    for load in loads:
        load.start()

    rows, span = checkpoint.shape[1:]
    half = span - LANES
    row = lax.broadcasted_iota(jnp.int32, (rows, span), 0)
    lane = lax.broadcasted_iota(jnp.int32, (rows, span), 1)
    z = lax.bitwise_and(lane, NZ - 1)
    first_z, last_z = z == 0, z == NZ - 1
    row_h = lax.broadcasted_iota(jnp.int32, (rows, LANES), 0)
    lane_h = lax.broadcasted_iota(jnp.int32, (rows, LANES), 1)
    slot_h = lax.shift_right_logical(lane_h, 4)
    row_t = lax.broadcasted_iota(jnp.int32, (NTURB, LANES), 0)
    lane_t = lax.broadcasted_iota(jnp.int32, (NTURB, LANES), 1)

    def turned(value, shift, axis):
        shift = shift % value.shape[axis]
        return pltpu.roll(value, shift, axis) if shift else value

    def edge_of(sign):
        return rows - 1 if sign == 1 else 0

    def rim_lane(sign):
        return LANES - NZ if sign == 1 else 0

    def side_of(value, sign):
        return value[:, half:] if sign == 1 else value[:, :LANES]

    def pack_x(values, sign):
        packed = jnp.zeros((rows, span), jnp.float32)
        for k, value in enumerate(values):
            packed = jnp.where(row == k, turned(value, k - edge_of(sign), 0), packed)
        return packed

    def pack_y(values, sign):
        packed = jnp.zeros((rows, LANES), jnp.float32)
        for k, value in enumerate(values):
            moved = turned(side_of(value, sign), NZ * k - rim_lane(sign), 1)
            packed = jnp.where(slot_h == k, moved, packed)
        return packed

    def send_halo(f, fields, e, greeted=None):
        for sign, start in ((1, 0), (-1, 2)):
            packed = pack_x([f[i] for i in moving(0, sign)] + fields, sign)
            halo_out[e, start] = packed[:, :LANES]
            halo_out[e, start + 1] = packed[:, half:]
        for sign, start in ((1, 4), (-1, 5)):
            halo_out[e, start] = pack_y([f[i] for i in moving(1, sign)] + fields, sign)
            for dx in (1, -1):
                edge = edge_of(dx)
                turn_out[e, CORNER[(dx, sign)]] = halo_out[e, start, edge : edge + 1]
        if greeted is not None:
            pl.semaphore_wait(barrier, greeted)
        send_rims(halo_out.at[e], halo_in.at[e], turn_out.at[e], turn_in.at[e], 1,
                  (halo_sent.at[0], halo_got.at[e], turn_sent.at[0], turn_got.at[e]))

    def send_rims(out, into, turn, into_turn, scale, sems):
        for rims, source, target, sent, got in ((RIMS, out, into) + sems[:2], (CORNERS, turn, into_turn) + sems[2:]):
            for where, slot, count in merged(rims, nx, ny):
                part = pl.ds(scale * slot, scale * count)
                pltpu.make_async_remote_copy(
                    src_ref=source.at[part], dst_ref=target.at[part], send_sem=sent, recv_sem=got,
                    device_id=at(*where), device_id_type=MESH).start()

    def receive(e, count):
        pltpu.make_async_copy(halo_in.at[e], halo_in.at[e], halo_got.at[e]).wait()
        pltpu.make_async_copy(turn_in.at[e], turn_in.at[e], turn_got.at[e]).wait()
        from_x, from_y = {}, {}
        fields_x = [None] * count
        fields_y = [jnp.zeros((rows, LANES), jnp.float32)] * count
        for sign, start in ((1, 0), (-1, 2)):
            got = jnp.concatenate([halo_in[e, start], halo_in[e, start + 1]], axis=1)
            for k, i in enumerate(moving(0, sign)):
                from_x[i] = turned(got, edge_of(sign) - k, 0)
            for k in range(count):
                value = turned(got, edge_of(sign) - 5 - k, 0)
                fields_x[k] = value if sign == 1 else jnp.where(row == 0, value, fields_x[k])
        for side, (dx, dy) in enumerate(SIDES):
            got = halo_in[e, 4 if dy == 1 else 5]
            if dx:
                got = jnp.where(row_h == edge_of(dx), turn_in[e, CORNER[(dx, dy)]], got)
            for k, i in enumerate(moving(1, dy)):
                if VEC[i][0] == dx:
                    from_y[i] = turned(got, rim_lane(dy) - NZ * k, 1)
            for k in range(count):
                value = turned(got, NZ * (side - 5 - k), 1)
                fields_y[k] = jnp.where(slot_h == side, value, fields_y[k])
        return from_x, from_y, fields_x, fields_y

    def run(f, from_x, from_y):
        out = {}
        for i in f:
            dx, dy, dz = VEC[i]
            value = f[i]
            if dx:
                value = jnp.where(row == edge_of(dx), from_x[i], value)
            if dy == 1:
                edge = jnp.where(lane_h >= LANES - NZ, from_y[i], value[:, half:])
                value = jnp.concatenate([value[:, :half], edge], axis=1)
            elif dy == -1:
                edge = jnp.where(lane_h < NZ, from_y[i], value[:, :LANES])
                value = jnp.concatenate([edge, value[:, LANES:]], axis=1)
            value = turned(turned(value, dx, 0), NZ * dy + dz, 1)
            if dz:
                value = jnp.where(first_z if dz == 1 else last_z, f[OPP[i]], value)
            out[i] = value
        return out

    def pulls_of(rate):
        lines = [jnp.broadcast_to(rate[t : t + 1], (rows, LANES)) for t in range(NTURB)]
        wides = [jnp.concatenate([line] * (span // LANES), axis=1) for line in lines]
        return (total([spread[t] * wides[t] for t in range(NTURB)]),
                total([ext_x[t] * wides[t] for t in range(NTURB)]),
                total([ext_y[t] * lines[t] for t in range(NTURB)]))

    def run_added(entries, correct, fields, fields_x, fields_y, pulls):
        add = correct(fields, [p[0] for p in pulls])
        add_x = correct(fields_x, [p[1] for p in pulls])
        add_y = correct(fields_y, [p[2] for p in pulls])
        from_x = {i: add_x(i) for i in entries if VEC[i][0]}
        from_y = {}
        for side, (dx, dy) in enumerate(SIDES):
            inside = [i for i in entries if VEC[i][:2] == (dx, dy)]
            if inside:
                value = turned(add_y(inside[0]), rim_lane(dy) - NZ * side, 1)
                from_y.update({i: value for i in inside})
        return run({i: add(i) for i in entries}, from_x, from_y)

    def row_sums(values):
        for step in (4, 2, 1):
            low_rows = lax.bitwise_and(row_h, step) == 0
            merged_values = []
            for a, b in zip(values[:step], values[step:]):
                kept, given = jnp.where(low_rows, a, b), jnp.where(low_rows, b, a)
                back = pltpu.roll(given, rows - step, 0)
                if step < 4:
                    back = jnp.where(low_rows, back, pltpu.roll(given, step, 0))
                merged_values.append(kept + back)
            values = merged_values
        return values[0]

    def turbine_sums(value):
        prods = [spread[t] * value for t in range(NTURB)]
        prods = [p[:, :LANES] + p[:, half:] for p in prods]
        sums = jnp.concatenate([row_sums(prods[:8]), row_sums(prods[8:])], axis=0)
        return jnp.broadcast_to(jnp.sum(sums, axis=1, keepdims=True), (NTURB, LANES))

    def send_partials(sums, e):
        width = LANES // (NTURB * len(sums))
        packed = jnp.zeros((NTURB, LANES), jnp.float32)
        for c, value in enumerate(sums):
            packed = jnp.where(lane_t // width == row_t + NTURB * c, value, packed)
        part_out[e] = jnp.sum(packed, axis=0, keepdims=True)
        for k, (dx, dy) in enumerate(near):
            pltpu.make_async_remote_copy(
                src_ref=part_out.at[e], dst_ref=part_in.at[e, k],
                send_sem=part_sent.at[0], recv_sem=part_got.at[e],
                device_id=at(dx, dy), device_id_type=MESH).start()

    def take_partials(count, e):
        width = LANES // (NTURB * count)
        pltpu.make_async_copy(part_in.at[e], part_in.at[e], part_got.at[e]).wait()
        both = total([part_out[e]] + [part_in[e, k] for k in range(len(near))])
        both = jnp.broadcast_to(both, (NTURB, LANES))
        out = []
        for c in range(count):
            picked = jnp.where(lane_t == width * (row_t + NTURB * c), both, 0.0)
            line = jnp.sum(picked, axis=1, keepdims=True)
            out.append(jnp.broadcast_to(line, (NTURB, LANES)) / denom)
        return out

    def wide(value, t):
        line = jnp.broadcast_to(value[t : t + 1], (rows, LANES))
        return jnp.concatenate([line] * (span // LANES), axis=1)

    def onehots(t):
        index = cell[t : t + 1, :]
        across = lax.shift_right_arithmetic(index, 8)
        along = lax.bitwise_and(index, 255)
        pick_x = lax.broadcasted_iota(jnp.int32, (rows, LANES), 0) == across
        pick_j = lax.broadcasted_iota(jnp.int32, (span, LANES), 0) == along
        return pick_x, jnp.where(pick_j, 1.0, 0.0).astype(jnp.bfloat16)

    def at_points(fields):
        lines = []
        for t in range(NTURB):
            pick_x, pick_j = onehots(t)
            found = join_thirds(jnp.dot(thirds(fields(t)), pick_j, preferred_element_type=jnp.float32))
            lines.append(jnp.sum(jnp.where(pick_x, found, 0.0), axis=0, keepdims=True))
        return jnp.concatenate(lines, axis=0)

    def sum_first(value, r):
        sum_out[r, 0] = value
        for k, (a, b) in enumerate(group):
            pltpu.make_async_remote_copy(
                src_ref=sum_out.at[r, 0], dst_ref=sum_a.at[r, k], send_sem=sum_sent.at[2 * r],
                recv_sem=sum_got.at[2 * r], device_id=in_group(a, b), device_id_type=MESH).start()

    def sum_second(r):
        pltpu.make_async_copy(sum_a.at[r], sum_a.at[r], sum_got.at[2 * r]).wait()
        sum_out[r, 1] = total([sum_out[r, 0]] + [sum_a[r, k] for k in range(len(group))])
        for k, c in enumerate(far):
            pltpu.make_async_remote_copy(
                src_ref=sum_out.at[r, 1], dst_ref=sum_b.at[r, k], send_sem=sum_sent.at[2 * r + 1],
                recv_sem=sum_got.at[2 * r + 1], device_id=in_far(c), device_id_type=MESH).start()

    def sum_last(r):
        pltpu.make_async_copy(sum_b.at[r], sum_b.at[r], sum_got.at[2 * r + 1]).wait()
        return total([sum_out[r, 1]] + [sum_b[r, k] for k in range(len(far))])

    loads[0].wait()
    field = [checkpoint[i] for i in range(19)]
    send_halo(field, [], 0, len(targets))

    def by_turbine(value):
        lines = []
        for t in range(NTURB):
            line, first = divmod(PTS * t, LANES)
            here = value[line : line + 1]
            if first + PTS > LANES:
                here = jnp.where(lane_t[:1] >= first, here, value[line + 1 : line + 2])
            lines.append(turned(here, -first, 1))
        return jnp.concatenate(lines, axis=0)

    def in_a_row(value):
        lines = []
        for line in range(NTURB * PTS // LANES):
            t, first = divmod(LANES * line, PTS)
            count = PTS - first
            after = turned(value[t + 1 : t + 2], count, 1)
            lines.append(jnp.where(lane_t[:1] < count, turned(value[t : t + 1], -first, 1), after))
        return jnp.concatenate(lines, axis=0)

    for load in loads[1:5]:
        load.wait()
    code = by_turbine(flat_side[...] * (rows * span) + flat_local[...])
    side = lax.shift_right_logical(code, 11)
    side_x = jnp.where(side >= 6, 2, jnp.where(side >= 3, 1, 0))
    side_y = side - 3 * side_x
    off_x, off_y = side_x - 1, side_y - 1
    hub_x, hub_y = jnp.zeros_like(side), jnp.zeros_like(side)
    for t in range(NTURB):
        hub = hubs[t]
        hub_x = jnp.where(row_t == t, lax.div(hub, ny) - ix, hub_x)
        hub_y = jnp.where(row_t == t, lax.rem(hub, ny) - iy, hub_y)
    off_x, off_y = off_x + hub_x, off_y + hub_y
    mine = (off_x == 0) | (off_x == nx) | (off_x == -nx)
    mine = mine & ((off_y == 0) | (off_y == ny) | (off_y == -ny)) & (lane_t < PTS)
    cell[...] = jnp.where(mine, lax.bitwise_and(code, rows * span - 1), -1)
    area[...] = jnp.where(lane_t < PTS, by_turbine(flat_area[...]), 0.0)

    for t in range(NTURB):
        pick_x, pick_j = onehots(t)
        weight = jnp.where(pick_x, area[t : t + 1, :], 0.0)
        spread[t] = join_thirds(lax.dot_general(
            thirds(weight), pick_j, (((1,), (1,)), ((), ())), preferred_element_type=jnp.float32))
    denom = jnp.broadcast_to(jnp.sum(area[...], axis=1, keepdims=True), (NTURB, LANES))
    for h in range(2):
        mine = [spread[8 * h + k] for k in range(8)]
        for sign, start in ((1, 0), (-1, 4)):
            packed = pack_x(mine, sign)
            rim_out[start + 2 * h] = packed[:, :LANES]
            rim_out[start + 2 * h + 1] = packed[:, half:]
        for sign, start in ((1, 8), (-1, 10)):
            rim_out[start + h] = pack_y(mine, sign)
    for sign, start in ((1, 8), (-1, 10)):
        for dx in (1, -1):
            for h in range(2):
                edge = edge_of(dx)
                rim_turn_out[2 * CORNER[(dx, sign)] + h] = rim_out[start + h, edge : edge + 1]
    send_rims(rim_out, rim_in, rim_turn_out, rim_turn_in, 2,
              (rim_sent.at[0], rim_got.at[0], rim_sent.at[1], rim_got.at[1]))

    def extend_spread():
        pltpu.make_async_copy(rim_in, rim_in, rim_got.at[0]).wait()
        pltpu.make_async_copy(rim_turn_in, rim_turn_in, rim_got.at[1]).wait()
        sides = []
        for dx, dy in SIDES:
            pair = []
            for h in range(2):
                value = rim_in[(8 if dy == 1 else 10) + h]
                if dx:
                    corner = rim_turn_in[2 * CORNER[(dx, dy)] + h]
                    value = jnp.where(row_h == edge_of(dx), corner, value)
                pair.append(value)
            sides.append(pair)
        for h in range(2):
            ups = jnp.concatenate([rim_in[2 * h], rim_in[2 * h + 1]], axis=1)
            downs = jnp.concatenate([rim_in[4 + 2 * h], rim_in[5 + 2 * h]], axis=1)
            for k in range(8):
                up, down = turned(ups, rows - 1 - k, 0), turned(downs, -k, 0)
                ext_x[8 * h + k] = jnp.where(row == rows - 1, up, jnp.where(row == 0, down, 0.0))
                packed = jnp.zeros((rows, LANES), jnp.float32)
                for side, pair in enumerate(sides):
                    moved = turned(pair[h], NZ * (side - k), 1)
                    packed = jnp.where(slot_h == side, moved, packed)
                ext_y[8 * h + k] = packed

    def forced(fields, pulls):
        force = -THRUST * fields[0] * pulls[0]
        return lambda i: PUSH[i] * force

    def speed_fixed(fields, pulls):
        speed_bar = fields[1] * pulls[0] + fields[2] * pulls[1]
        parts = {c: (float(-c) - fields[0]) * speed_bar for c in (-1, 0, 1)}
        return lambda i: parts[VEC[i][0]]

    rotors, speeds, pulls = [], [], []
    from_x, from_y, unused_x, unused_y = receive(0, 0)
    flat = run(dict(enumerate(field)), from_x, from_y)
    pushed_on = [i for i in range(19) if PUSH[i] != 0.0]
    for s in range(STEPS):
        flat = [flat[i] for i in range(19)]
        for i in range(19):
            flats[s, i] = flat[i]
        speed = momentum_of(flat, 0) / density_of(flat)
        speeds.append(speed)
        if s == STEPS - 1:
            break
        send_partials([turbine_sums(speed)], s)
        moved = collide(*flat)
        send_halo(moved, [speed], s + 1)
        if s == 0:
            extend_spread()
        from_x, from_y, fields_x, fields_y = receive(s + 1, 1)
        flat = run(dict(enumerate(moved)), from_x, from_y)
        rotors.append(take_partials(1, s)[0])
        pulls.append(pulls_of(rotors[s]))
        added = run_added(pushed_on, forced, [speed], fields_x, fields_y, [pulls[s]])
        flat.update({i: flat[i] + added[i] for i in pushed_on})

    loads[5].wait()
    adjoint = [cotangent[i] for i in range(19)]
    for n in range(STEPS):
        s, e = STEPS - 1 - n, STEPS + n
        flat = [flats[s, i] for i in range(19)]
        speed = speeds[s]
        force_bar = weighted(PUSH, adjoint)
        load = -THRUST * force_bar * speed
        load_sums = turbine_sums(load)
        if n == 0:
            send_partials([turbine_sums(speed), load_sums], s)
        else:
            send_partials([load_sums], s + 2 * n)
        if n == STEPS - 1:
            rotor = rotors[s]
            found = at_points(lambda t: grads[t] + wide(rotor, t) * load)
            sum_first(jnp.where(lane_t < PTS, found, load_sums), 1)
        unused, pullback = jax.vjp(collide, *flat)
        flat_bar = pullback(tuple(adjoint))
        inverse = 1.0 / density_of(flat)
        fields = [speed, inverse, -THRUST * force_bar * inverse]
        turned_bar = [flat_bar[OPP[i]] for i in range(19)]
        send_halo(turned_bar, fields, e)
        if n == 0:
            sum_first(at_points(lambda t: speeds[0] - wide(rotors[0], t)), 0)
        elif n == 1:
            sum_second(0)
        if n == STEPS - 1:
            sum_second(1)
        from_x, from_y, fields_x, fields_y = receive(e, 3)
        pushed = run(dict(enumerate(turned_bar)), from_x, from_y)
        if n == 0:
            rotor, numer_bar = take_partials(2, s)
            pulls.append(pulls_of(rotor))
        else:
            rotor = rotors[s]
            numer_bar = take_partials(1, s + 2 * n)[0]
        added = run_added(range(19), speed_fixed, fields, fields_x, fields_y, [pulls_of(numer_bar), pulls[s]])
        adjoint = [pushed[OPP[i]] + added[OPP[i]] for i in range(19)]
        if n < STEPS - 1:
            for t in range(NTURB):
                turn = wide(rotor, t)
                part = turn * load + wide(numer_bar, t) * (speed - turn)
                grads[t] = part if n == 0 else grads[t] + part

    for i in range(19):
        checkpoint[i] = adjoint[i]
    store = pltpu.make_async_copy(checkpoint, grad, loaded.at[0])
    store.start()
    spread_of = sum_last(0)
    sums = sum_last(1)
    numer_bar = jnp.broadcast_to(sums[:, PTS : PTS + 1], (NTURB, LANES)) / denom
    area_grad[...] = in_a_row(sums + numer_bar * spread_of)
    store.wait()

    pltpu.make_async_copy(halo_in, halo_in, halo_sent.at[0]).wait()
    pltpu.make_async_copy(turn_in, turn_in, turn_sent.at[0]).wait()
    pltpu.make_async_copy(part_in, part_in, part_sent.at[0]).wait()
    pltpu.make_async_copy(rim_in, rim_in, rim_sent.at[0]).wait()
    pltpu.make_async_copy(rim_turn_in, rim_turn_in, rim_sent.at[1]).wait()
    for r in range(2):
        pltpu.make_async_copy(sum_a.at[r], sum_a.at[r], sum_sent.at[2 * r]).wait()
        pltpu.make_async_copy(sum_b.at[r], sum_b.at[r], sum_sent.at[2 * r + 1]).wait()


def body(checkpoint, cotangent, blade_area, hub_tile, point_side, point_local):
    nx, ny = lax.axis_size("gx"), lax.axis_size("gy")
    pops, rows, span = checkpoint.shape
    lines = (NTURB * PTS // LANES, LANES)
    near = len(near_offsets(nx, REACH)) * len(near_offsets(ny, REACH)) - 1
    group, far = SUBCELLS * ny - 1, nx // SUBCELLS - 1
    f32, dma = jnp.float32, pltpu.SemaphoreType.DMA
    tile, vreg = (rows, span), (rows, LANES)
    ints = [pltpu.SMEM((NTURB,), jnp.int32), pltpu.VMEM(lines, f32)]
    ints += [pltpu.VMEM(lines, jnp.int32)] * 2
    ints += [pltpu.VMEM((NTURB, LANES), f32), pltpu.VMEM((NTURB, LANES), jnp.int32)]
    shapes = [(STEPS, pops) + tile] + [(NTURB,) + tile] * 3 + [(NTURB,) + vreg]
    shapes += [(HALOS, 6) + vreg] * 2 + [(12,) + vreg] * 2
    shapes += [(HALOS, 4, 1, LANES)] * 2 + [(8, 1, LANES)] * 2
    shapes += [(PARTIALS, 1, LANES), (PARTIALS, near, 1, LANES)]
    shapes += [(2, 2, NTURB, LANES), (2, group, NTURB, LANES), (2, far, NTURB, LANES)]
    whole = pl.BlockSpec(memory_space=pltpu.VMEM)
    adjoint, grads = pl.pallas_call(
        functools.partial(kernel, nx, ny),
        out_shape=(jax.ShapeDtypeStruct(checkpoint.shape, f32),
                   jax.ShapeDtypeStruct(lines, f32)),
        in_specs=[pl.BlockSpec(memory_space=pltpu.HBM)] * 6,
        out_specs=(pl.BlockSpec(memory_space=pltpu.HBM), whole),
        scratch_shapes=[pltpu.VMEM((pops,) + tile, f32)] * 2 + ints
        + [pltpu.VMEM(shape, f32) for shape in shapes]
        + [dma((HALOS,))] * 2 + [dma((2,))] * 2 + [dma((HALOS,))] * 2 + [dma((PARTIALS,))] * 2 + [dma((4,))] * 2 + [dma((6,))],
        compiler_params=pltpu.CompilerParams(
            collective_id=0, has_side_effects=True, vmem_limit_bytes=60 * 1024 * 1024),
    )(checkpoint, cotangent, hub_tile, blade_area.reshape(lines), point_side.reshape(lines), point_local.reshape(lines))
    return adjoint, grads.reshape(NTURB * PTS)


def solution(mesh):
    return jax.shard_map(
        body,
        mesh=mesh,
        in_specs=(P(None, "gx", "gy"), P(None, "gx", "gy"), P(), P(), P(), P()),
        out_specs=(P(None, "gx", "gy"), P()),
        check_vma=False,
    )
```
